512 devices in a mesh: section: 32 (over z, y_hi), tensor: 16 (over x, y_lo, core).
Axes of the slice: x: 4, y: 8 (y_hi: 4, y_lo: 2; y = y_hi * 2 + y_lo), z: 8, core: 2. Of those that a mesh axis runs over, the one named last changes fastest.
Arguments:
- down_batch_input: bfloat16 [8, 64, 4096], P(None, None, 'tensor'), may hold values from -6 to 6
- up_batch_input: bfloat16 [8, 64, 4096], P(None, None, 'tensor'), may hold values from -6 to 6
- down_relay_lower_weight: bfloat16 [32, 4096, 64], P('section', 'tensor'), may hold values from -0.09375 to 0.09375
- down_relay_upper_weight: bfloat16 [32, 64, 4096], P('section', None, 'tensor'), may hold values from -0.1875 to 0.1875
- up_relay_lower_weight: bfloat16 [32, 4096, 64], P('section', 'tensor'), may hold values from -0.09375 to 0.09375
- up_relay_upper_weight: bfloat16 [32, 64, 4096], P('section', None, 'tensor'), may hold values from -0.1875 to 0.1875
- frozen_down_weight: bfloat16 [32, 4096, 4096], P('section', None, 'tensor'), may hold values from -0.046875 to 0.046875
- frozen_up_weight: bfloat16 [32, 4096, 4096], P('section', None, 'tensor'), may hold values from -0.046875 to 0.046875
Outputs:
- grad_a_down: float32 [32, 4096, 64], P('section', 'tensor')
- grad_b_down: float32 [32, 64, 4096], P('section', None, 'tensor')
- grad_a_up: float32 [32, 4096, 64], P('section', 'tensor')
- grad_b_up: float32 [32, 64, 4096], P('section', None, 'tensor')
The draws below stay inside these ranges and needn't reach their ends.
All inputs are finite; a program needn't handle non-finite values.
Results may differ from the reference program's by a relative error of at most 0.014.
Values may be sent and summed in bfloat16 or wider, within the bound.
A program may use at most 64 MiB of HBM per device.

```python
import jax
import jax.numpy as jnp

MODEL_WIDTH = 4096
ADAPTER_RANK = 64
TOK = 64
RELAY_LAYERS = 4
SECTION_LAYERS = 32
PIPES = 8


def levels(key, dims, split, smallest, top_value):
    def one(axis_at, blocks):
        draws = jax.random.uniform(jax.random.fold_in(jax.random.fold_in(key, 6), axis_at), (blocks,), jnp.float32, smallest / len(split), top_value / len(split))
        return jnp.repeat(jnp.exp(draws), dims[axis_at] // blocks).reshape((-1,) + (1,) * (len(dims) - axis_at - 1))

    factor_of = one(*split[0])
    for cut in split[1:]:
        factor_of = factor_of * one(*cut)
    return factor_of


def bell_draw(rng, shape, deviation, reach, split=(), dtype=jnp.bfloat16):
    drawn = jax.random.normal(rng, shape, jnp.float32) * deviation
    if len(split) > 0:
        drawn = levels(rng, shape, split, -0.22, 0.18) * drawn
    return jnp.clip(drawn, min=-reach, max=reach).astype(dtype)


def setup_inputs(seed: int = 0) -> dict:
    keys = jax.random.split(jax.random.key(seed), 9)
    down_batch_input = bell_draw(keys[0], (PIPES, TOK, MODEL_WIDTH), 1.0, 6.0, ((2, 16),))
    up_batch_input = bell_draw(keys[1], (PIPES, TOK, MODEL_WIDTH), 1.0, 6.0, ((2, 16),))
    down_relay_lower_weight = bell_draw(keys[2], (SECTION_LAYERS, MODEL_WIDTH, ADAPTER_RANK), MODEL_WIDTH ** -0.5, 0.09375, ((0, 32), (1, 16)))
    down_relay_upper_weight = bell_draw(keys[3], (SECTION_LAYERS, ADAPTER_RANK, MODEL_WIDTH), ((4 * ADAPTER_RANK * RELAY_LAYERS) ** -0.5), 0.1875, ((0, 32), (2, 16)))
    up_relay_lower_weight = bell_draw(keys[4], (SECTION_LAYERS, MODEL_WIDTH, ADAPTER_RANK), MODEL_WIDTH ** -0.5, 0.09375, ((0, 32), (1, 16)))
    up_relay_upper_weight = bell_draw(keys[5], (SECTION_LAYERS, ADAPTER_RANK, MODEL_WIDTH), ((4 * ADAPTER_RANK * RELAY_LAYERS) ** -0.5), 0.1875, ((0, 32), (2, 16)))
    frozen_down_weight = bell_draw(keys[6], (SECTION_LAYERS, MODEL_WIDTH, MODEL_WIDTH), (0.5 * MODEL_WIDTH ** -0.5), 0.046875, ((0, 32), (2, 16)))
    frozen_up_weight = bell_draw(keys[7], (SECTION_LAYERS, MODEL_WIDTH, MODEL_WIDTH), (0.5 * MODEL_WIDTH ** -0.5), 0.046875, ((0, 32), (2, 16)))
    return {"down_batch_input": down_batch_input, "up_batch_input": up_batch_input, "down_relay_lower_weight": down_relay_lower_weight, "down_relay_upper_weight": down_relay_upper_weight, "up_relay_lower_weight": up_relay_lower_weight, "up_relay_upper_weight": up_relay_upper_weight, "frozen_down_weight": frozen_down_weight, "frozen_up_weight": frozen_up_weight}


SCALE = 2.0


def layer_number(hidden_state, w, a, b):
    c = (SCALE * jnp.dot(hidden_state, a, preferred_element_type=jnp.float32)).astype(jnp.bfloat16)
    out = hidden_state.astype(jnp.float32) + jnp.dot(hidden_state, w, preferred_element_type=jnp.float32) + jnp.dot(c, b, preferred_element_type=jnp.float32)
    return out.astype(jnp.bfloat16), c


def backward_pass(hidden_state, c, error_signal, w, a, b):
    g = jnp.dot(error_signal, b.T, preferred_element_type=jnp.float32).astype(jnp.bfloat16)
    grad_a = SCALE * jnp.dot(hidden_state.T, g, preferred_element_type=jnp.float32)
    grad_b = jnp.dot(c.T, error_signal, preferred_element_type=jnp.float32)
    e_prev = error_signal.astype(jnp.float32) + jnp.dot(error_signal, w.T, preferred_element_type=jnp.float32) + SCALE * jnp.dot(g, a.T, preferred_element_type=jnp.float32)
    return e_prev.astype(jnp.bfloat16), grad_a, grad_b


def reference(down_batch_input, up_batch_input, down_relay_lower_weight, down_relay_upper_weight, up_relay_lower_weight, up_relay_upper_weight, frozen_down_weight, frozen_up_weight):
    layer_count = down_relay_lower_weight.shape[0]
    groups = down_batch_input.shape[0]
    span = layer_count // groups
    gradient_lower_down, gradient_upper_down, gradient_lower_up, gradient_upper_up = [None] * layer_count, [None] * layer_count, [None] * layer_count, [None] * layer_count
    for p in range(groups):
        layer_offset = p * span
        down_layer_input, down_coefficient_rows = [None] * span, [None] * span
        hidden_state = down_batch_input[p]
        for section_index in range(span):
            down_layer_input[section_index] = hidden_state
            hidden_state, down_coefficient_rows[section_index] = layer_number(hidden_state, frozen_down_weight[layer_offset + section_index], down_relay_lower_weight[layer_offset + section_index], down_relay_upper_weight[layer_offset + section_index])
        up_layer_input, up_coefficient_rows = [None] * span, [None] * span
        relay_position = up_batch_input[p]
        for section_index in range(span - 1, -1, -1):
            up_layer_input[section_index] = relay_position
            relay_position, up_coefficient_rows[section_index] = layer_number(relay_position, frozen_up_weight[layer_offset + section_index], up_relay_lower_weight[layer_offset + section_index], up_relay_upper_weight[layer_offset + section_index])
        error_signal = hidden_state
        for section_index in range(span - 1, -1, -1):
            error_signal, gradient_lower_down[layer_offset + section_index], gradient_upper_down[layer_offset + section_index] = backward_pass(down_layer_input[section_index], down_coefficient_rows[section_index], error_signal, frozen_down_weight[layer_offset + section_index], down_relay_lower_weight[layer_offset + section_index], down_relay_upper_weight[layer_offset + section_index])
        error_signal = relay_position
        for section_index in range(span):
            error_signal, gradient_lower_up[layer_offset + section_index], gradient_upper_up[layer_offset + section_index] = backward_pass(up_layer_input[section_index], up_coefficient_rows[section_index], error_signal, frozen_up_weight[layer_offset + section_index], up_relay_lower_weight[layer_offset + section_index], up_relay_upper_weight[layer_offset + section_index])
    return (jnp.stack(gradient_lower_down), jnp.stack(gradient_upper_down), jnp.stack(gradient_lower_up), jnp.stack(gradient_upper_up))
```

```python
import functools

import jax
import jax.numpy as jnp
from jax import lax
from jax.experimental import pallas as pl
from jax.experimental.pallas import tpu as pltpu
from jax.sharding import PartitionSpec as P

MESH = pl.DeviceIdType.MESH
F32, BF16 = jnp.float32, jnp.bfloat16
LAYERS = 4
CHIPS = 8
TOK = 64
COLS = 256
RANK = 64
SPLIT = 2
ROWS = TOK // SPLIT
SCALE = 2.0
FAR = (5, 4, 7, 3, 6, 2, 1)
NEAR = (0, 1, 2, 6, 3, 7, 4, 5)


def nn(a, b):
    return jnp.dot(a, b, preferred_element_type=F32)


def nt(a, b):
    return lax.dot_general(a, b, (((1,), (1,)), ((), ())), preferred_element_type=F32)


def tn(a, b):
    return lax.dot_general(a, b, (((0,), (0,)), ((), ())), preferred_element_type=F32)


def fold(v):
    return jnp.concatenate([v[: TOK // 2], v[TOK // 2 :]], axis=1)


def unfold(v):
    return jnp.concatenate([v[:, :RANK], v[:, RANK:]], axis=0)


def kernel(
    xd, xu, atd, atu, bd, bu, wd, wu,
    gad, gbd, gau, gbu,
    w, weff, at, bch, hb, xs, xp, hout, eb, ps, pr, eout, gs, gr, cs, cr,
    ld_x, ld_a, ld_b, ld_w,
    w_s, w_r, b_s, b_r, a_s, a_r, h_s, h_r, hx_s, hx_r, hc_s, hc_r,
    ec_s, ec_r, ex_s, ex_r, p_s, p_r, g_s, g_r, c_s, c_r,
):
    sec, t = lax.axis_index("section"), lax.axis_index("tensor")
    group, s = sec // LAYERS, sec % LAYERS
    chip, core = t // 2, t % 2
    low = s < 2
    q1 = jnp.where(low, s, LAYERS - 1 - s)
    toward = jnp.where(low, 1, -1)
    sibling = (sec, t ^ 1)

    def peer(m):
        return (sec, t ^ (2 * m))

    def rows(i):
        return pl.ds(i * ROWS, ROWS)

    def remote(src, dst, send, recv, to):
        return pltpu.make_async_remote_copy(
            src_ref=src, dst_ref=dst, send_sem=send, recv_sem=recv,
            device_id=to, device_id_type=MESH,
        )

    def start_local(r, down):
        x, a, b, v = (xd, atd, bd, wd) if down else (xu, atu, bu, wu)
        if r == 0:

            @pl.when(q1 == 0)
            def _():
                pltpu.make_async_copy(x.at[group], hb.at[0, 0], ld_x).start()

        pltpu.make_async_copy(a, at.at[r, 0], ld_a.at[r]).start()
        pltpu.make_async_copy(b, bch.at[r, 0], ld_b.at[r]).start()
        pltpu.make_async_copy(v.at[:, core], w.at[r, 0], ld_w.at[r]).start()

    @pl.when(low)
    def _():
        start_local(0, True)
        start_local(1, False)

    @pl.when(jnp.logical_not(low))
    def _():
        start_local(0, False)
        start_local(1, True)

    barrier = pltpu.get_barrier_semaphore()
    for m in range(1, CHIPS):
        pl.semaphore_signal(barrier, inc=1, device_id=peer(m), device_id_type=MESH)
    pl.semaphore_signal(barrier, inc=1, device_id=sibling, device_id_type=MESH)

    @pl.when(s > 0)
    def _():
        pl.semaphore_signal(barrier, inc=1, device_id=(sec - 1, t), device_id_type=MESH)

    @pl.when(s < LAYERS - 1)
    def _():
        pl.semaphore_signal(barrier, inc=1, device_id=(sec + 1, t), device_id_type=MESH)

    pl.semaphore_wait(barrier, jnp.where(q1 == 0, CHIPS + 1, CHIPS + 2))

    def h_copy(r, i, m):
        return remote(
            hb.at[r, 0, rows(i)], hb.at[r, m, rows(i)], h_s.at[r, i, m], h_r.at[r, i, m], peer(m)
        )

    def a_copy(r, m):
        return remote(at.at[r, 0], at.at[r, m], a_s.at[r, m], a_r.at[r, m], peer(m))

    def b_copy(r):
        return remote(bch.at[r, 0], bch.at[r, 1], b_s.at[r], b_r.at[r], sibling)

    def w_copy(r, down):
        v = wd if down else wu
        return remote(v.at[:, 1 - core], w.at[r, 1], w_s.at[r], w_r.at[r], sibling)

    @pl.when(q1 == 0)
    def _():
        pltpu.make_async_copy(xd.at[group], hb.at[0, 0], ld_x).wait()
        for i in range(SPLIT):
            for m in FAR:
                h_copy(0, i, m).start()

    def share_weights(r):
        pltpu.make_async_copy(atd, at.at[r, 0], ld_a.at[r]).wait()
        for m in FAR:
            a_copy(r, m).start()

        @pl.when(low == (r == 0))
        def _():
            w_copy(r, True).start()

        @pl.when(low != (r == 0))
        def _():
            w_copy(r, False).start()

        pltpu.make_async_copy(bd, bch.at[r, 0], ld_b.at[r]).wait()
        b_copy(r).start()

    share_weights(0)
    share_weights(1)

    def combine_weights(r):
        b_copy(r).wait_recv()
        pltpu.make_async_copy(wd.at[:, core], w.at[r, 0], ld_w.at[r]).wait()
        w_copy(r, True).wait_recv()
        for m in NEAR:
            if m:
                a_copy(r, m).wait_recv()
            j = chip ^ m
            for half in range(2):
                low_rank = tn(at[r, m], bch[r, half])
                weff[r, j, :, half * COLS : (half + 1) * COLS] = (
                    w[r, half, j].astype(F32) + SCALE * low_rank
                ).astype(BF16)

    def hx_copy(r, i):
        return remote(xs.at[r, rows(i)], xp.at[r, rows(i)], hx_s.at[r, i], hx_r.at[r, i], sibling)

    def hc_copy(r, i):
        to = (sec + toward, t) if r == 0 else (sec - toward, t)
        there = q1 if r == 0 else 1
        return remote(
            hout.at[r, rows(i)], hb.at[there, 0, rows(i)], hc_s.at[r, i], hc_r.at[there, i], to
        )

    def hc_arrived(r, i):
        remote(
            hout.at[r, rows(i)], hb.at[r, 0, rows(i)], hc_s.at[r, i], hc_r.at[r, i], sibling
        ).wait_recv()

    def gather(r):
        for i in range(SPLIT):
            hc_arrived(r, i)
            for m in FAR:
                h_copy(r, i, m).start()

    def forward(r):
        own = []
        for i in range(SPLIT):
            total = jnp.zeros((ROWS, 2 * COLS), F32)
            for m in NEAR:
                if m:
                    h_copy(r, i, m).wait_recv()
                total = total + nn(hb[r, m, i * ROWS : (i + 1) * ROWS], weff[r, chip ^ m])
            xs[r, i * ROWS : (i + 1) * ROWS] = total[:, COLS:]
            hx_copy(r, i).start()
            own.append(total[:, :COLS])
        for i in range(SPLIT):
            piece = slice(i * ROWS, (i + 1) * ROWS)
            hx_copy(r, i).wait_recv()
            out = (hb[r, 0, piece].astype(F32) + own[i] + xp[r, piece]).astype(BF16)
            if r == 0:
                hout[r, piece] = out
                hc_copy(r, i).start()
            else:

                @pl.when(q1 == 1)
                def _():
                    hout[r, piece] = out
                    hc_copy(r, i).start()

                @pl.when(q1 == 0)
                def _():
                    eb[r, 0, piece] = out

    def c_copy(r):
        return remote(cs.at[r], cr.at[r], c_s.at[r], c_r.at[r], sibling)

    def coefficients(r):
        total = nt(hb[r, 0], at[r, 0])
        for m in range(1, CHIPS):
            total = total + nt(hb[r, m], at[r, m])
        cs[r] = fold(SCALE * total)
        c_copy(r).start()

    def drain_forward(r):
        for i in range(SPLIT):
            for m in FAR:
                h_copy(r, i, m).wait_send()
            hx_copy(r, i).wait_send()
            if r == 0:
                hc_copy(r, i).wait_send()
            else:

                @pl.when(q1 == 1)
                def _():
                    hc_copy(r, i).wait_send()

    def drain_weights(r):
        for m in FAR:
            a_copy(r, m).wait_send()
        b_copy(r).wait_send()
        w_copy(r, True).wait_send()

    combine_weights(0)

    @pl.when(q1 == 1)
    def _():
        gather(0)

    forward(0)
    combine_weights(1)
    coefficients(0)
    drain_weights(0)
    drain_weights(1)
    drain_forward(0)

    gather(1)
    forward(1)

    def ec_copy(r, i):
        to = (sec - toward, t) if r == 0 else (sec + toward, t)
        there = 0 if r == 0 else 1 - q1
        return remote(
            eout.at[r, rows(i)], eb.at[there, 0, rows(i)], ec_s.at[r, i], ec_r.at[there, i], to
        )

    def ec_arrived(r, i):
        remote(
            eout.at[r, rows(i)], eb.at[r, 0, rows(i)], ec_s.at[r, i], ec_r.at[r, i], sibling
        ).wait_recv()

    def ex_copy(r, i):
        return remote(
            eb.at[r, 0, rows(i)], eb.at[r, 1, rows(i)], ex_s.at[r, i], ex_r.at[r, i], sibling
        )

    def p_copy(r, i, m):
        return remote(
            ps.at[r, m, rows(i)], pr.at[r, m, rows(i)], p_s.at[r, i, m], p_r.at[r, i, m], peer(m)
        )

    def g_copy(r, m):
        return remote(gs.at[r], gr.at[r, m], g_s.at[r, m], g_r.at[r, m], peer(m))

    def arrive(r):
        for i in range(SPLIT):
            if r == 0:
                ec_arrived(r, i)
            else:

                @pl.when(q1 == 1)
                def _():
                    ec_arrived(r, i)

            ex_copy(r, i).start()

    def sum_g(r):
        total = nt(eb[r, 0], bch[r, 0]) + nt(eb[r, 1], bch[r, 1])
        gs[r] = fold(total)
        for m in FAR:
            g_copy(r, m).start()

    def backward(r):
        own = []
        for i in range(SPLIT):
            piece = slice(i * ROWS, (i + 1) * ROWS)
            e_own, e_other = eb[r, 0, piece], eb[r, 1, piece]
            for m in FAR + (0,):
                block = weff.at[r, chip ^ m]
                part = nt(e_own, block[:, :COLS]) + nt(e_other, block[:, COLS:])
                if m:
                    ps[r, m, piece] = part.astype(BF16)
                    p_copy(r, i, m).start()
                else:
                    own.append(part)
        for i in range(SPLIT):
            piece = slice(i * ROWS, (i + 1) * ROWS)
            total = eb[r, 0, piece].astype(F32) + own[i]
            for m in NEAR[1:]:
                p_copy(r, i, m).wait_recv()
                total = total + pr[r, m, piece].astype(F32)
            eout[r, piece] = total.astype(BF16)
            ec_copy(r, i).start()

    def drain_backward(r):
        for i in range(SPLIT):
            for m in FAR:
                p_copy(r, i, m).wait_send()
            ec_copy(r, i).wait_send()

    def finish(r):
        c_copy(r).wait_recv()
        c = unfold(cs[r] + cr[r]).astype(BF16)
        grad_b = tn(c, eb[r, 0])
        total = gs[r]
        for m in NEAR[1:]:
            g_copy(r, m).wait_recv()
            total = total + gr[r, m]
        g = unfold(total).astype(BF16)
        grad_a = SCALE * tn(g, hb[r, 0])

        @pl.when(low == (r == 0))
        def _():
            gad[...] = grad_a
            gbd[...] = grad_b

        @pl.when(low != (r == 0))
        def _():
            gau[...] = grad_a
            gbu[...] = grad_b

    def arrived_other(r):
        for i in range(SPLIT):
            ex_copy(r, i).wait_recv()

    arrive(1)
    arrived_other(1)
    backward(1)
    sum_g(1)
    coefficients(1)
    drain_forward(1)
    finish(1)
    drain_backward(1)

    arrive(0)
    arrived_other(0)

    @pl.when(q1 == 1)
    def _():
        backward(0)

    sum_g(0)
    finish(0)

    @pl.when(q1 == 1)
    def _():
        drain_backward(0)

    for r in range(2):
        for i in range(SPLIT):
            ex_copy(r, i).wait_send()
        for m in FAR:
            g_copy(r, m).wait_send()
        c_copy(r).wait_send()


def body(xd, xu, ad, bd, au, bu, wd, wu):
    def chunks(v):
        return v.reshape(CHIPS, 2, COLS, COLS)

    dma = pltpu.SemaphoreType.DMA
    anywhere = pl.BlockSpec(memory_space=pl.ANY)
    vmem = pl.BlockSpec(memory_space=pltpu.VMEM)
    pair = dma((2,))
    halves = dma((2, SPLIT))
    each = dma((2, SPLIT, CHIPS))
    chips = dma((2, CHIPS))
    gad, gbd, gau, gbu = pl.pallas_call(
        kernel,
        out_shape=[jax.ShapeDtypeStruct((RANK, COLS), F32)] * 4,
        in_specs=[anywhere] * 8,
        out_specs=[vmem] * 4,
        scratch_shapes=[
            pltpu.VMEM((2, 2, CHIPS, COLS, COLS), BF16),
            pltpu.VMEM((2, CHIPS, COLS, 2 * COLS), BF16),
            pltpu.VMEM((2, CHIPS, RANK, COLS), BF16),
            pltpu.VMEM((2, 2, RANK, COLS), BF16),
            pltpu.VMEM((2, CHIPS, TOK, COLS), BF16),
            pltpu.VMEM((2, TOK, COLS), F32),
            pltpu.VMEM((2, TOK, COLS), F32),
            pltpu.VMEM((2, TOK, COLS), BF16),
            pltpu.VMEM((2, 2, TOK, COLS), BF16),
            pltpu.VMEM((2, CHIPS, TOK, COLS), BF16),
            pltpu.VMEM((2, CHIPS, TOK, COLS), BF16),
            pltpu.VMEM((2, TOK, COLS), BF16),
            pltpu.VMEM((2, TOK // 2, 2 * RANK), F32),
            pltpu.VMEM((2, CHIPS, TOK // 2, 2 * RANK), F32),
            pltpu.VMEM((2, TOK // 2, 2 * RANK), F32),
            pltpu.VMEM((2, TOK // 2, 2 * RANK), F32),
            dma, pair, pair, pair,
            pair, pair, pair, pair, chips, chips,
            each, each, halves, halves, halves, halves,
            halves, halves, halves, halves,
            each, each, chips, chips, pair, pair,
        ],
        compiler_params=pltpu.CompilerParams(
            collective_id=0, has_side_effects=True, vmem_limit_bytes=40 * 2**20
        ),
        cost_estimate=pl.CostEstimate(
            flops=8 * TOK * LAYERS * 1024 * COLS, bytes_accessed=6 * 2**20, transcendentals=0
        ),
    )(
        xd, xu, ad[0].T, au[0].T, bd[0], bu[0], chunks(wd), chunks(wu)
    )
    return gad.T[None], gbd[None], gau.T[None], gbu[None]


def solution(mesh):
    in_specs = (
        P(None, None, "tensor"),
        P(None, None, "tensor"),
        P("section", "tensor", None),
        P("section", None, "tensor"),
        P("section", "tensor", None),
        P("section", None, "tensor"),
        P("section", None, "tensor"),
        P("section", None, "tensor"),
    )
    out_specs = (
        P("section", "tensor", None),
        P("section", None, "tensor"),
        P("section", "tensor", None),
        P("section", None, "tensor"),
    )
    return jax.shard_map(body, mesh=mesh, in_specs=in_specs, out_specs=out_specs, check_vma=False)
```

```python
import functools

import jax
import jax.numpy as jnp
from jax import lax
from jax.experimental import pallas as pl
from jax.experimental.pallas import tpu as pltpu
from jax.sharding import PartitionSpec as P

MESH = pl.DeviceIdType.MESH
F32, BF16 = jnp.float32, jnp.bfloat16
LAYERS = 4
CHIPS = 8
TOK = 64
COLS = 256
RANK = 64
SPLIT = 2
ROWS = TOK // SPLIT
SCALE = 2.0
FAR = (5, 4, 7, 3, 6, 2, 1)
NEAR = (0, 1, 2, 6, 3, 7, 4, 5)


def nn(a, b):
    return jnp.dot(a, b, preferred_element_type=F32)


def nt(a, b):
    return lax.dot_general(a, b, (((1,), (1,)), ((), ())), preferred_element_type=F32)


def tn(a, b):
    return lax.dot_general(a, b, (((0,), (0,)), ((), ())), preferred_element_type=F32)


def fold(v):
    return jnp.concatenate([v[: TOK // 2], v[TOK // 2 :]], axis=1)


def unfold(v):
    return jnp.concatenate([v[:, :RANK], v[:, RANK:]], axis=0)


def kernel(
    xd, xu, atd, atu, bd, bu, wd, wu,
    c_out, g_out, h_out, e_out,
    w, weff, at, bch, hb, xs, xp, ts, tp, hout, eb, ps, pr, eout, gs, gr, cs, cr, fs, fr,
    ld_x, ld_a, ld_b, ld_w,
    w_s, w_r, b_s, b_r, a_s, a_r, h_s, h_r, hx_s, hx_r, hc_s, hc_r,
    ec_s, ec_r, ex_s, ex_r, p_s, p_r, g_s, g_r, c_s, c_r, t_s, t_r, f_s, f_r,
):
    sec, t = lax.axis_index("section"), lax.axis_index("tensor")
    group, s = sec // LAYERS, sec % LAYERS
    chip, core = t // 2, t % 2
    low = s < 2
    q1 = jnp.where(low, s, LAYERS - 1 - s)
    toward = jnp.where(low, 1, -1)
    sibling = (sec, t ^ 1)

    def peer(m):
        return (sec, t ^ (2 * m))

    def rows(i):
        return pl.ds(i * ROWS, ROWS)

    def remote(src, dst, send, recv, to):
        return pltpu.make_async_remote_copy(
            src_ref=src, dst_ref=dst, send_sem=send, recv_sem=recv,
            device_id=to, device_id_type=MESH,
        )

    def start_local(r, down):
        x, a, b, v = (xd, atd, bd, wd) if down else (xu, atu, bu, wu)
        if r == 0:

            @pl.when(q1 == 0)
            def _():
                pltpu.make_async_copy(x.at[group], hb.at[0, 0], ld_x).start()

        pltpu.make_async_copy(a, at.at[r, 0], ld_a.at[r]).start()
        pltpu.make_async_copy(b, bch.at[r, 0], ld_b.at[r]).start()
        pltpu.make_async_copy(v.at[:, core], w.at[r, 0], ld_w.at[r]).start()

    @pl.when(low)
    def _():
        start_local(0, True)
        start_local(1, False)

    @pl.when(jnp.logical_not(low))
    def _():
        start_local(0, False)
        start_local(1, True)

    barrier = pltpu.get_barrier_semaphore()
    for m in range(1, CHIPS):
        pl.semaphore_signal(barrier, inc=1, device_id=peer(m), device_id_type=MESH)
    pl.semaphore_signal(barrier, inc=1, device_id=sibling, device_id_type=MESH)

    @pl.when(s > 0)
    def _():
        pl.semaphore_signal(barrier, inc=1, device_id=(sec - 1, t), device_id_type=MESH)

    @pl.when(s < LAYERS - 1)
    def _():
        pl.semaphore_signal(barrier, inc=1, device_id=(sec + 1, t), device_id_type=MESH)

    pl.semaphore_wait(barrier, jnp.where(q1 == 0, CHIPS + 1, CHIPS + 2))

    def h_copy(r, i, m):
        return remote(
            hb.at[r, 0, rows(i)], hb.at[r, m, rows(i)], h_s.at[r, i, m], h_r.at[r, i, m], peer(m)
        )

    def a_copy(r, m):
        return remote(at.at[r, 0], at.at[r, m], a_s.at[r, m], a_r.at[r, m], peer(m))

    def b_copy(r):
        return remote(bch.at[r, 0], bch.at[r, 1], b_s.at[r], b_r.at[r], sibling)

    def w_copy(r, down):
        v = wd if down else wu
        return remote(v.at[:, 1 - core], w.at[r, 1], w_s.at[r], w_r.at[r], sibling)

    @pl.when(q1 == 0)
    def _():
        pltpu.make_async_copy(xd.at[group], hb.at[0, 0], ld_x).wait()
        for i in range(SPLIT):
            for m in FAR:
                h_copy(0, i, m).start()

    def f_copy(m):
        return remote(fs, fr.at[m], f_s.at[m], f_r.at[m], peer(m))

    for r in range(2):
        pltpu.make_async_copy(atd, at.at[r, 0], ld_a.at[r]).wait()

    @pl.when(q1 == 0)
    def _():
        fs[...] = fold(SCALE * nt(hb[0, 0], at[0, 0]))
        for m in FAR:
            f_copy(m).start()

    def share_lower(r):
        for m in FAR:
            a_copy(r, m).start()

    def share_weights(r):
        @pl.when(low == (r == 0))
        def _():
            w_copy(r, True).start()

        @pl.when(low != (r == 0))
        def _():
            w_copy(r, False).start()

        pltpu.make_async_copy(bd, bch.at[r, 0], ld_b.at[r]).wait()
        b_copy(r).start()

    share_weights(0)

    @pl.when(q1 == 1)
    def _():
        share_lower(0)
        share_lower(1)

    share_weights(1)

    def weights_here(r):
        b_copy(r).wait_recv()
        pltpu.make_async_copy(wd.at[:, core], w.at[r, 0], ld_w.at[r]).wait()
        w_copy(r, True).wait_recv()

    def combine_weights(r):
        for m in NEAR:
            if m:
                a_copy(r, m).wait_recv()
            j = chip ^ m
            for half in range(2):
                low_rank = tn(at[r, m], bch[r, half])
                weff[r, j, :, half * COLS : (half + 1) * COLS] = (
                    w[r, half, j].astype(F32) + SCALE * low_rank
                ).astype(BF16)

    def hx_copy(r, i):
        return remote(xs.at[r, rows(i)], xp.at[r, rows(i)], hx_s.at[r, i], hx_r.at[r, i], sibling)

    def hc_copy(r, i):
        to = (sec + toward, t) if r == 0 else (sec - toward, t)
        there = q1 if r == 0 else 1
        return remote(
            hout.at[r, rows(i)], hb.at[there, 0, rows(i)], hc_s.at[r, i], hc_r.at[there, i], to
        )

    def hc_arrived(r, i):
        remote(
            hout.at[r, rows(i)], hb.at[r, 0, rows(i)], hc_s.at[r, i], hc_r.at[r, i], sibling
        ).wait_recv()

    def gather(r):
        for i in range(SPLIT):
            hc_arrived(r, i)
            for m in FAR:
                h_copy(r, i, m).start()

    def t_copy(i):
        return remote(ts.at[rows(i)], tp.at[rows(i)], t_s.at[i], t_r.at[i], sibling)

    def first_layer():
        lower = fs[...]
        for m in NEAR[1:]:
            f_copy(m).wait_recv()
            lower = lower + fr[m]
        cs[0] = lower
        c_copy(0).start()
        c = unfold(lower).astype(BF16)
        halves = []
        for i in range(SPLIT):
            piece = slice(i * ROWS, (i + 1) * ROWS)
            own, other = nn(c[piece], bch[0, 0]), nn(c[piece], bch[0, 1])
            for m in NEAR:
                if m:
                    h_copy(0, i, m).wait_recv()
                other = other + nn(hb[0, m, piece], w[0, 1, chip ^ m])
            xs[0, piece] = other
            hx_copy(0, i).start()
            for m in NEAR:
                own = own + nn(hb[0, m, piece], w[0, 0, chip ^ m])
            halves.append(own)
        for i in range(SPLIT):
            piece = slice(i * ROWS, (i + 1) * ROWS)
            hx_copy(0, i).wait_recv()
            out = (hb[0, 0, piece].astype(F32) + halves[i] + xp[0, piece]).astype(BF16)
            hout[0, piece] = out
            hc_copy(0, i).start()

    def later_layer(r, last):
        own, other = [], []
        for i in range(SPLIT):
            piece = slice(i * ROWS, (i + 1) * ROWS)
            total = jnp.zeros((ROWS, 2 * COLS), F32)
            for m in NEAR:
                if m:
                    h_copy(r, i, m).wait_recv()
                total = total + nn(hb[r, m, piece], weff[r, chip ^ m])
            xs[r, piece] = total[:, COLS:]
            hx_copy(r, i).start()
            mine = hb[r, 0, piece].astype(F32) + total[:, :COLS]
            if last:
                ts[piece] = mine
                t_copy(i).start()
            own.append(mine)
            other.append(total[:, COLS:])
        for i in range(SPLIT):
            piece = slice(i * ROWS, (i + 1) * ROWS)
            hx_copy(r, i).wait_recv()
            out = (own[i] + xp[r, piece]).astype(BF16)
            if last:
                eb[r, 0, piece] = out
                t_copy(i).wait_recv()
                eb[r, 1, piece] = (other[i] + tp[piece]).astype(BF16)
            else:
                hout[r, piece] = out
                hc_copy(r, i).start()

    def c_copy(r):
        return remote(cs.at[r], cr.at[r], c_s.at[r], c_r.at[r], sibling)

    def coefficients(r):
        total = nt(hb[r, 0], at[r, 0])
        for m in range(1, CHIPS):
            total = total + nt(hb[r, m], at[r, m])
        cs[r] = fold(SCALE * total)
        c_copy(r).start()

    def drain_forward(r):
        for i in range(SPLIT):
            for m in FAR:
                h_copy(r, i, m).wait_send()
            hx_copy(r, i).wait_send()
            if r == 1:

                @pl.when(q1 == 0)
                def _():
                    t_copy(i).wait_send()

            if r == 0:
                hc_copy(r, i).wait_send()
            else:

                @pl.when(q1 == 1)
                def _():
                    hc_copy(r, i).wait_send()

    def drain_weights(r):
        if r == 1:
            for m in FAR:
                a_copy(r, m).wait_send()
        b_copy(r).wait_send()
        w_copy(r, True).wait_send()

    weights_here(0)

    @pl.when(q1 == 0)
    def _():
        first_layer()
        share_lower(1)
        for m in FAR:
            f_copy(m).wait_send()

    @pl.when(q1 == 1)
    def _():
        combine_weights(0)
        gather(0)
        later_layer(0, False)
        coefficients(0)
        for m in FAR:
            a_copy(0, m).wait_send()

    weights_here(1)
    combine_weights(1)
    drain_weights(0)
    drain_weights(1)
    drain_forward(0)

    gather(1)

    @pl.when(q1 == 0)
    def _():
        later_layer(1, True)

    @pl.when(q1 == 1)
    def _():
        later_layer(1, False)

    def ec_copy(r, i):
        to = (sec - toward, t) if r == 0 else (sec + toward, t)
        there = 0 if r == 0 else 1 - q1
        return remote(
            eout.at[r, rows(i)], eb.at[there, 0, rows(i)], ec_s.at[r, i], ec_r.at[there, i], to
        )

    def ec_arrived(r, i):
        remote(
            eout.at[r, rows(i)], eb.at[r, 0, rows(i)], ec_s.at[r, i], ec_r.at[r, i], sibling
        ).wait_recv()

    def ex_copy(r, i):
        return remote(
            eb.at[r, 0, rows(i)], eb.at[r, 1, rows(i)], ex_s.at[r, i], ex_r.at[r, i], sibling
        )

    def p_copy(r, i, m):
        return remote(
            ps.at[r, m, rows(i)], pr.at[r, m, rows(i)], p_s.at[r, i, m], p_r.at[r, i, m], peer(m)
        )

    def g_copy(r, m):
        return remote(gs.at[r], gr.at[r, m], g_s.at[r, m], g_r.at[r, m], peer(m))

    def arrive(r):
        for i in range(SPLIT):
            ec_arrived(r, i)
            ex_copy(r, i).start()
        for i in range(SPLIT):
            ex_copy(r, i).wait_recv()

    def sum_g(r):
        total = nt(eb[r, 0], bch[r, 0]) + nt(eb[r, 1], bch[r, 1])
        gs[r] = fold(total)
        for m in FAR:
            g_copy(r, m).start()

    def backward(r):
        own = []
        for i in range(SPLIT):
            piece = slice(i * ROWS, (i + 1) * ROWS)
            e_own, e_other = eb[r, 0, piece], eb[r, 1, piece]
            for m in FAR + (0,):
                block = weff.at[r, chip ^ m]
                part = nt(e_own, block[:, :COLS]) + nt(e_other, block[:, COLS:])
                if m:
                    ps[r, m, piece] = part.astype(BF16)
                    p_copy(r, i, m).start()
                else:
                    own.append(part)
        for i in range(SPLIT):
            piece = slice(i * ROWS, (i + 1) * ROWS)
            total = eb[r, 0, piece].astype(F32) + own[i]
            for m in NEAR[1:]:
                p_copy(r, i, m).wait_recv()
                total = total + pr[r, m, piece].astype(F32)
            eout[r, piece] = total.astype(BF16)
            ec_copy(r, i).start()

    def drain_backward(r):
        for i in range(SPLIT):
            for m in FAR:
                p_copy(r, i, m).wait_send()
            ec_copy(r, i).wait_send()

    def finish(r):
        c_copy(r).wait_recv()
        c_out[r] = unfold(cs[r] + cr[r]).astype(BF16)
        h_out[r] = hb[r, 0]
        e_out[r] = eb[r, 0]
        total = gs[r]
        for m in NEAR[1:]:
            g_copy(r, m).wait_recv()
            total = total + gr[r, m]
        g_out[r] = unfold(total).astype(BF16)

    @pl.when(q1 == 1)
    def _():
        arrive(1)

    backward(1)
    sum_g(1)
    coefficients(1)
    drain_forward(1)
    finish(1)
    drain_backward(1)

    arrive(0)

    @pl.when(q1 == 1)
    def _():
        backward(0)

    sum_g(0)
    finish(0)

    @pl.when(q1 == 1)
    def _():
        drain_backward(0)
        for i in range(SPLIT):
            ex_copy(1, i).wait_send()

    for i in range(SPLIT):
        ex_copy(0, i).wait_send()
    for r in range(2):
        for m in FAR:
            g_copy(r, m).wait_send()
        c_copy(r).wait_send()


def gradients(c, g, h, e, gad, gbd, gau, gbu):
    low = lax.axis_index("section") % LAYERS < 2
    grad_a = [SCALE * tn(g[r], h[r]) for r in range(2)]
    grad_b = [tn(c[r], e[r]) for r in range(2)]

    @pl.when(low)
    def _():
        gad[...], gbd[...], gau[...], gbu[...] = grad_a[0], grad_b[0], grad_a[1], grad_b[1]

    @pl.when(jnp.logical_not(low))
    def _():
        gad[...], gbd[...], gau[...], gbu[...] = grad_a[1], grad_b[1], grad_a[0], grad_b[0]


def body(xd, xu, ad, bd, au, bu, wd, wu):
    def chunks(v):
        return v.reshape(CHIPS, 2, COLS, COLS)

    dma = pltpu.SemaphoreType.DMA
    anywhere = pl.BlockSpec(memory_space=pltpu.HBM)
    vmem = pl.BlockSpec(memory_space=pltpu.VMEM)
    pair = dma((2,))
    halves = dma((2, SPLIT))
    each = dma((2, SPLIT, CHIPS))
    chips = dma((2, CHIPS))
    parts = pl.pallas_call(
        kernel,
        out_shape=[jax.ShapeDtypeStruct((2, TOK, n), BF16) for n in (RANK, RANK, COLS, COLS)],
        in_specs=[anywhere] * 8,
        out_specs=[vmem] * 4,
        scratch_shapes=[
            pltpu.VMEM((2, 2, CHIPS, COLS, COLS), BF16),
            pltpu.VMEM((2, CHIPS, COLS, 2 * COLS), BF16),
            pltpu.VMEM((2, CHIPS, RANK, COLS), BF16),
            pltpu.VMEM((2, 2, RANK, COLS), BF16),
            pltpu.VMEM((2, CHIPS, TOK, COLS), BF16),
            pltpu.VMEM((2, TOK, COLS), F32),
            pltpu.VMEM((2, TOK, COLS), F32),
            pltpu.VMEM((TOK, COLS), F32),
            pltpu.VMEM((TOK, COLS), F32),
            pltpu.VMEM((2, TOK, COLS), BF16),
            pltpu.VMEM((2, 2, TOK, COLS), BF16),
            pltpu.VMEM((2, CHIPS, TOK, COLS), BF16),
            pltpu.VMEM((2, CHIPS, TOK, COLS), BF16),
            pltpu.VMEM((2, TOK, COLS), BF16),
            pltpu.VMEM((2, TOK // 2, 2 * RANK), F32),
            pltpu.VMEM((2, CHIPS, TOK // 2, 2 * RANK), F32),
            pltpu.VMEM((2, TOK // 2, 2 * RANK), F32),
            pltpu.VMEM((2, TOK // 2, 2 * RANK), F32),
            pltpu.VMEM((TOK // 2, 2 * RANK), F32),
            pltpu.VMEM((CHIPS, TOK // 2, 2 * RANK), F32),
            dma, pair, pair, pair,
            pair, pair, pair, pair, chips, chips,
            each, each, halves, halves, halves, halves,
            halves, halves, halves, halves,
            each, each, chips, chips, pair, pair,
            dma((SPLIT,)), dma((SPLIT,)), dma((CHIPS,)), dma((CHIPS,)),
        ],
        compiler_params=pltpu.CompilerParams(
            collective_id=0, has_side_effects=True, vmem_limit_bytes=62 * 2**20
        ),
        cost_estimate=pl.CostEstimate(
            flops=8 * TOK * LAYERS * 1024 * COLS, bytes_accessed=6 * 2**20, transcendentals=0
        ),
    )(
        xd, xu, ad[0].T, au[0].T, bd[0], bu[0], chunks(wd), chunks(wu)
    )
    gad, gbd, gau, gbu = pl.pallas_call(
        gradients,
        out_shape=[jax.ShapeDtypeStruct((RANK, COLS), F32)] * 4,
        in_specs=[vmem] * 4,
        out_specs=[vmem] * 4,
        compiler_params=pltpu.CompilerParams(vmem_limit_bytes=62 * 2**20),
    )(*parts)
    return gad.T[None], gbd[None], gau.T[None], gbu[None]


def solution(mesh):
    in_specs = (
        P(None, None, "tensor"),
        P(None, None, "tensor"),
        P("section", "tensor", None),
        P("section", None, "tensor"),
        P("section", "tensor", None),
        P("section", None, "tensor"),
        P("section", None, "tensor"),
        P("section", None, "tensor"),
    )
    out_specs = (
        P("section", "tensor", None),
        P("section", None, "tensor"),
        P("section", "tensor", None),
        P("section", None, "tensor"),
    )
    return jax.shard_map(body, mesh=mesh, in_specs=in_specs, out_specs=out_specs, check_vma=False)
```

```python
import functools

import jax
import jax.numpy as jnp
from jax import lax
from jax.experimental import pallas as pl
from jax.experimental.pallas import tpu as pltpu
from jax.sharding import PartitionSpec as P

MESH = pl.DeviceIdType.MESH
F32, BF16 = jnp.float32, jnp.bfloat16
LAYERS = 4
CHIPS = 8
TOK = 64
COLS = 256
RANK = 64
SPLIT = 2
ROWS = TOK // SPLIT
SCALE = 2.0
FAR = (5, 4, 7, 3, 6, 2, 1)
NEAR = (0, 1, 2, 6, 3, 7, 4, 5)
WIDE = (11, 10, 9, 8, 15, 14, 7, 6, 13, 12, 5, 4, 3, 2, 1)


def nn(a, b):
    return jnp.dot(a, b, preferred_element_type=F32)


def nt(a, b):
    return lax.dot_general(a, b, (((1,), (1,)), ((), ())), preferred_element_type=F32)


def tn(a, b):
    return lax.dot_general(a, b, (((0,), (0,)), ((), ())), preferred_element_type=F32)


def fold(v):
    return jnp.concatenate([v[: TOK // 2], v[TOK // 2 :]], axis=1)


def unfold(v):
    return jnp.concatenate([v[:, :RANK], v[:, RANK:]], axis=0)


def kernel(
    xd, xu, atd, atu, bd, bu, wd, wu,
    c_out, g_out, h_out, e_out,
    w, weff, at, bch, hb, xs, xp, ts, tp, hout, eb, ps, pr, eout, gs, gr, cs, cr, fs, fr,
    kept, b0, bp, us, ur, vs, vr,
    ld_x, ld_a, ld_b, ld_w,
    w_s, w_r, b_s, b_r, a_s, a_r, h_s, h_r, hx_s, hx_r, hc_s, hc_r,
    ec_s, ec_r, ex_s, ex_r, p_s, p_r, g_s, g_r, c_s, c_r, t_s, t_r, f_s, f_r,
    n_s, n_r, m_s, m_r, u_s, u_r, v_s, v_r,
):
    sec, t = lax.axis_index("section"), lax.axis_index("tensor")
    group, s = sec // LAYERS, sec % LAYERS
    chip, core = t // 2, t % 2
    low = s < 2
    q1 = jnp.where(low, s, LAYERS - 1 - s)
    toward = jnp.where(low, 1, -1)
    sibling = (sec, t ^ 1)

    def peer(m):
        return (sec, t ^ (2 * m))

    def rows(i):
        return pl.ds(i * ROWS, ROWS)

    def remote(src, dst, send, recv, to):
        return pltpu.make_async_remote_copy(
            src_ref=src, dst_ref=dst, send_sem=send, recv_sem=recv,
            device_id=to, device_id_type=MESH,
        )

    def start_local(r, down):
        x, a, b, v = (xd, atd, bd, wd) if down else (xu, atu, bu, wu)
        if r == 0:

            @pl.when(q1 == 0)
            def _():
                pltpu.make_async_copy(x.at[group], hb.at[0, 0], ld_x).start()

        pltpu.make_async_copy(a, at.at[r, 0], ld_a.at[r]).start()
        pltpu.make_async_copy(b, bch.at[r, 0], ld_b.at[r]).start()
        pltpu.make_async_copy(v.at[:, core], w.at[r, 0], ld_w.at[r]).start()

    @pl.when(low)
    def _():
        start_local(0, True)
        start_local(1, False)

    @pl.when(jnp.logical_not(low))
    def _():
        start_local(0, False)
        start_local(1, True)

    barrier = pltpu.get_barrier_semaphore()
    for m in range(1, CHIPS):
        pl.semaphore_signal(barrier, inc=1, device_id=peer(m), device_id_type=MESH)
    pl.semaphore_signal(barrier, inc=1, device_id=sibling, device_id_type=MESH)

    @pl.when(s > 0)
    def _():
        pl.semaphore_signal(barrier, inc=1, device_id=(sec - 1, t), device_id_type=MESH)

    @pl.when(s < LAYERS - 1)
    def _():
        pl.semaphore_signal(barrier, inc=1, device_id=(sec + 1, t), device_id_type=MESH)

    pl.semaphore_wait(barrier, jnp.where(q1 == 0, CHIPS + 1, CHIPS + 2))

    def h_copy(r, i, m):
        return remote(
            hb.at[r, 0, rows(i)], hb.at[r, m, rows(i)], h_s.at[r, i, m], h_r.at[r, i, m], peer(m)
        )

    def a_copy(r, m):
        return remote(at.at[r, 0], at.at[r, m], a_s.at[r, m], a_r.at[r, m], peer(m))

    def b_copy(r):
        return remote(bch.at[r, 0], bch.at[r, 1], b_s.at[r], b_r.at[r], sibling)

    def w_copy(r, down):
        v = wd if down else wu
        return remote(v.at[:, 1 - core], w.at[r, 1], w_s.at[r], w_r.at[r], sibling)

    @pl.when(q1 == 0)
    def _():
        pltpu.make_async_copy(xd.at[group], hb.at[0, 0], ld_x).wait()
        for i in range(SPLIT):
            for m in FAR:
                h_copy(0, i, m).start()

    def f_copy(m):
        return remote(fs, fr.at[m], f_s.at[m], f_r.at[m], peer(m))

    for r in range(2):
        pltpu.make_async_copy(atd, at.at[r, 0], ld_a.at[r]).wait()

    @pl.when(q1 == 0)
    def _():
        fs[...] = fold(SCALE * nt(hb[0, 0], at[0, 0]))
        for m in FAR:
            f_copy(m).start()

    def share_lower(r):
        for m in FAR:
            a_copy(r, m).start()

    def share_weights(r):
        @pl.when(low == (r == 0))
        def _():
            w_copy(r, True).start()

        @pl.when(low != (r == 0))
        def _():
            w_copy(r, False).start()

        pltpu.make_async_copy(bd, bch.at[r, 0], ld_b.at[r]).wait()
        b_copy(r).start()

    share_weights(0)

    @pl.when(q1 == 1)
    def _():
        share_lower(0)
        share_lower(1)

    share_weights(1)

    def weights_here(r):
        b_copy(r).wait_recv()
        pltpu.make_async_copy(wd.at[:, core], w.at[r, 0], ld_w.at[r]).wait()
        w_copy(r, True).wait_recv()

    def combine_weights(r):
        for m in NEAR:
            if m:
                a_copy(r, m).wait_recv()
            j = chip ^ m
            for half in range(2):
                low_rank = tn(at[r, m], bch[r, half])
                weff[r, j, :, half * COLS : (half + 1) * COLS] = (
                    w[r, half, j].astype(F32) + SCALE * low_rank
                ).astype(BF16)

    def hx_copy(r, i):
        return remote(xs.at[r, rows(i)], xp.at[r, rows(i)], hx_s.at[r, i], hx_r.at[r, i], sibling)

    def hc_copy(r, i):
        to = (sec + toward, t) if r == 0 else (sec - toward, t)
        there = q1 if r == 0 else 1
        return remote(
            hout.at[r, rows(i)], hb.at[there, 0, rows(i)], hc_s.at[r, i], hc_r.at[there, i], to
        )

    def hc_arrived(r, i):
        remote(
            hout.at[r, rows(i)], hb.at[r, 0, rows(i)], hc_s.at[r, i], hc_r.at[r, i], sibling
        ).wait_recv()

    def gather(r):
        for i in range(SPLIT):
            hc_arrived(r, i)
            for m in FAR:
                h_copy(r, i, m).start()

    def t_copy(i):
        return remote(ts.at[rows(i)], tp.at[rows(i)], t_s.at[i], t_r.at[i], sibling)

    def first_layer():
        lower = fs[...]
        for m in NEAR[1:]:
            f_copy(m).wait_recv()
            lower = lower + fr[m]
        cs[0] = lower
        c_copy(0).start()
        c = unfold(lower).astype(BF16)
        for i in range(SPLIT):
            piece = slice(i * ROWS, (i + 1) * ROWS)
            own, other = nn(c[piece], bch[0, 0]), nn(c[piece], bch[0, 1])
            for m in NEAR:
                if m:
                    h_copy(0, i, m).wait_recv()
                other = other + nn(hb[0, m, piece], w[0, 1, chip ^ m])
            xs[0, piece] = other
            hx_copy(0, i).start()
            for m in NEAR:
                own = own + nn(hb[0, m, piece], w[0, 0, chip ^ m])
            own = own + hb[0, 0, piece].astype(F32)
            hx_copy(0, i).wait_recv()
            hout[0, piece] = (own + xp[0, piece]).astype(BF16)
            hc_copy(0, i).start()

    def later_layer(r, i, last):
        piece = slice(i * ROWS, (i + 1) * ROWS)
        total = jnp.zeros((ROWS, 2 * COLS), F32)
        for m in NEAR:
            if m:
                h_copy(r, i, m).wait_recv()
            total = total + nn(hb[r, m, piece], weff[r, chip ^ m])
        xs[r, piece] = total[:, COLS:]
        hx_copy(r, i).start()
        mine = hb[r, 0, piece].astype(F32) + total[:, :COLS]
        if last:
            ts[piece] = mine
            t_copy(i).start()
        hx_copy(r, i).wait_recv()
        out = (mine + xp[r, piece]).astype(BF16)
        if last:
            eb[r, 0, piece] = out
            t_copy(i).wait_recv()
            eb[r, 1, piece] = (total[:, COLS:] + tp[piece]).astype(BF16)
        else:
            hout[r, piece] = out
            hc_copy(r, i).start()

    def c_copy(r):
        return remote(cs.at[r], cr.at[r], c_s.at[r], c_r.at[r], sibling)

    def coefficients(r):
        total = nt(hb[r, 0], at[r, 0])
        for m in range(1, CHIPS):
            total = total + nt(hb[r, m], at[r, m])
        cs[r] = fold(SCALE * total)
        c_copy(r).start()

    def drain_forward(r):
        for i in range(SPLIT):
            for m in FAR:
                h_copy(r, i, m).wait_send()
            hx_copy(r, i).wait_send()
            if r == 1:

                @pl.when(q1 == 0)
                def _():
                    t_copy(i).wait_send()

            if r == 0:
                hc_copy(r, i).wait_send()
            else:

                @pl.when(q1 == 1)
                def _():
                    hc_copy(r, i).wait_send()

    def drain_weights(r):
        if r == 1:
            for m in FAR:
                a_copy(r, m).wait_send()
        b_copy(r).wait_send()
        w_copy(r, True).wait_send()

    def ec_copy(r, i):
        to = (sec - toward, t) if r == 0 else (sec + toward, t)
        there = 0 if r == 0 else 1 - q1
        return remote(
            eout.at[r, rows(i)], eb.at[there, 0, rows(i)], ec_s.at[r, i], ec_r.at[there, i], to
        )

    def ec_arrived(r, i):
        remote(
            eout.at[r, rows(i)], eb.at[r, 0, rows(i)], ec_s.at[r, i], ec_r.at[r, i], sibling
        ).wait_recv()

    def ex_copy(r, i):
        return remote(
            eb.at[r, 0, rows(i)], eb.at[r, 1, rows(i)], ex_s.at[r, i], ex_r.at[r, i], sibling
        )

    def p_copy(r, i, m):
        return remote(
            ps.at[r, m, rows(i)], pr.at[r, m, rows(i)], p_s.at[r, i, m], p_r.at[r, i, m], peer(m)
        )

    def g_copy(r, m):
        return remote(gs.at[r], gr.at[r, m], g_s.at[r, m], g_r.at[r, m], peer(m))

    def sum_g(r):
        total = nt(eb[r, 0], bch[r, 0]) + nt(eb[r, 1], bch[r, 1])
        gs[r] = fold(total)
        for m in FAR:
            g_copy(r, m).start()

    def backward_out(r, i, turn):
        piece = slice(i * ROWS, (i + 1) * ROWS)
        if not turn:
            ec_arrived(r, i)
            ex_copy(r, i).start()
        e_own = eb[r, 0, piece]
        parts = [nt(e_own, weff[r, chip ^ m, :, :COLS]) for m in FAR + (0,)]
        if not turn:
            ex_copy(r, i).wait_recv()
        e_other = eb[r, 1, piece]
        for m, part in zip(FAR + (0,), parts):
            part = part + nt(e_other, weff[r, chip ^ m, :, COLS:])
            if m:
                ps[r, m, piece] = part.astype(BF16)
                p_copy(r, i, m).start()
            else:
                kept[r, piece] = part + e_own.astype(F32)

    def backward_in(r, i):
        piece = slice(i * ROWS, (i + 1) * ROWS)
        total = kept[r, piece]
        for m in NEAR[1:]:
            p_copy(r, i, m).wait_recv()
            total = total + pr[r, m, piece].astype(F32)
        eout[r, piece] = total.astype(BF16)
        ec_copy(r, i).start()

    def drain_backward(r):
        for i in range(SPLIT):
            for m in FAR:
                p_copy(r, i, m).wait_send()
            ec_copy(r, i).wait_send()

    def n_copy():
        return remote(bch.at[0, 0], b0.at[0], n_s, n_r, (sec + toward, t))

    def m_copy(m):
        return remote(b0.at[0], b0.at[m], m_s.at[m], m_r.at[m], peer(m))

    def u_copy():
        return remote(us, ur, u_s, u_r, (sec - toward, t))

    def v_copy(n):
        return remote(vs, vr.at[n], v_s.at[n], v_r.at[n], (sec, t ^ n))

    def prepare_ahead():
        remote(bch.at[0, 0], b0.at[0], n_s, n_r, sibling).wait_recv()
        for m in FAR:
            m_copy(m).start()
        own, other = b0[0].astype(F32), jnp.zeros((RANK, COLS), F32)
        for m in NEAR:
            if m:
                m_copy(m).wait_recv()
            own = own + nn(b0[m], weff[0, chip ^ m, :, :COLS])
            other = other + nn(b0[m], weff[0, chip ^ m, :, COLS:])
        bp[0] = own.astype(BF16)
        bp[1] = other.astype(BF16)
        for m in FAR:
            m_copy(m).wait_send()

    def send_ahead():
        us[...] = fold(nt(eb[0, 0], bp[0]) + nt(eb[0, 1], bp[1]))
        u_copy().start()

    def receive_ahead():
        remote(us, ur, u_s, u_r, sibling).wait_recv()
        vs[...] = ur[...].astype(BF16)
        for n in WIDE:
            v_copy(n).start()
        total = ur[...]
        for n in reversed(WIDE):
            v_copy(n).wait_recv()
            total = total + vr[n].astype(F32)
        g_out[0] = unfold(total).astype(BF16)

    def keep(r):
        c_copy(r).wait_recv()
        c_out[r] = unfold(cs[r] + cr[r]).astype(BF16)
        h_out[r] = hb[r, 0]

    def finish(r):
        total = gs[r]
        for m in NEAR[1:]:
            g_copy(r, m).wait_recv()
            total = total + gr[r, m]
        g_out[r] = unfold(total).astype(BF16)
        e_out[r] = eb[r, 0]

    def close_forward():
        drain_weights(0)
        drain_weights(1)
        drain_forward(0)
        keep(0)

    def close_backward(r):
        finish(r)
        drain_backward(r)
        for m in FAR:
            g_copy(r, m).wait_send()

    @pl.when(q1 == 0)
    def _():
        weights_here(0)
        first_layer()
        n_copy().start()
        share_lower(1)
        for m in FAR:
            f_copy(m).wait_send()
        weights_here(1)
        combine_weights(1)
        n_copy().wait_send()
        close_forward()
        gather(1)
        for i in range(SPLIT):
            later_layer(1, i, True)
            backward_out(1, i, True)
        for i in range(SPLIT):
            backward_in(1, i)
        sum_g(1)
        coefficients(1)
        drain_forward(1)
        keep(1)
        close_backward(1)
        receive_ahead()
        for n in WIDE:
            v_copy(n).wait_send()
        for i in range(SPLIT):
            ec_arrived(0, i)
        e_out[0] = eb[0, 0]

    @pl.when(q1 == 1)
    def _():
        weights_here(0)
        combine_weights(0)
        gather(0)
        weights_here(1)
        combine_weights(1)
        for i in range(SPLIT):
            later_layer(0, i, False)
        gather(1)
        coefficients(0)
        for m in FAR:
            a_copy(0, m).wait_send()
        close_forward()
        for i in range(SPLIT):
            later_layer(1, i, False)
        prepare_ahead()
        coefficients(1)
        drain_forward(1)
        keep(1)
        for i in range(SPLIT):
            backward_out(1, i, False)
        for i in range(SPLIT):
            backward_in(1, i)
        sum_g(1)
        for i in range(SPLIT):
            backward_out(0, i, False)
        send_ahead()
        close_backward(1)
        for i in range(SPLIT):
            backward_in(0, i)
        sum_g(0)
        close_backward(0)
        for r in range(2):
            for i in range(SPLIT):
                ex_copy(r, i).wait_send()
        u_copy().wait_send()

    for r in range(2):
        c_copy(r).wait_send()


def gradients(c, g, h, e, gad, gbd, gau, gbu):
    low = lax.axis_index("section") % LAYERS < 2
    grad_a = [SCALE * tn(g[r], h[r]) for r in range(2)]
    grad_b = [tn(c[r], e[r]) for r in range(2)]

    @pl.when(low)
    def _():
        gad[...], gbd[...], gau[...], gbu[...] = grad_a[0], grad_b[0], grad_a[1], grad_b[1]

    @pl.when(jnp.logical_not(low))
    def _():
        gad[...], gbd[...], gau[...], gbu[...] = grad_a[1], grad_b[1], grad_a[0], grad_b[0]


def body(xd, xu, ad, bd, au, bu, wd, wu):
    def chunks(v):
        return v.reshape(CHIPS, 2, COLS, COLS)

    dma = pltpu.SemaphoreType.DMA
    anywhere = pl.BlockSpec(memory_space=pltpu.HBM)
    vmem = pl.BlockSpec(memory_space=pltpu.VMEM)
    pair = dma((2,))
    halves = dma((2, SPLIT))
    each = dma((2, SPLIT, CHIPS))
    chips = dma((2, CHIPS))
    parts = pl.pallas_call(
        kernel,
        out_shape=[jax.ShapeDtypeStruct((2, TOK, n), BF16) for n in (RANK, RANK, COLS, COLS)],
        in_specs=[anywhere] * 8,
        out_specs=[vmem] * 4,
        scratch_shapes=[
            pltpu.VMEM((2, 2, CHIPS, COLS, COLS), BF16),
            pltpu.VMEM((2, CHIPS, COLS, 2 * COLS), BF16),
            pltpu.VMEM((2, CHIPS, RANK, COLS), BF16),
            pltpu.VMEM((2, 2, RANK, COLS), BF16),
            pltpu.VMEM((2, CHIPS, TOK, COLS), BF16),
            pltpu.VMEM((2, TOK, COLS), F32),
            pltpu.VMEM((2, TOK, COLS), F32),
            pltpu.VMEM((TOK, COLS), F32),
            pltpu.VMEM((TOK, COLS), F32),
            pltpu.VMEM((2, TOK, COLS), BF16),
            pltpu.VMEM((2, 2, TOK, COLS), BF16),
            pltpu.VMEM((2, CHIPS, TOK, COLS), BF16),
            pltpu.VMEM((2, CHIPS, TOK, COLS), BF16),
            pltpu.VMEM((2, TOK, COLS), BF16),
            pltpu.VMEM((2, TOK // 2, 2 * RANK), F32),
            pltpu.VMEM((2, CHIPS, TOK // 2, 2 * RANK), F32),
            pltpu.VMEM((2, TOK // 2, 2 * RANK), F32),
            pltpu.VMEM((2, TOK // 2, 2 * RANK), F32),
            pltpu.VMEM((TOK // 2, 2 * RANK), F32),
            pltpu.VMEM((CHIPS, TOK // 2, 2 * RANK), F32),
            pltpu.VMEM((2, TOK, COLS), F32),
            pltpu.VMEM((CHIPS, RANK, COLS), BF16),
            pltpu.VMEM((2, RANK, COLS), BF16),
            pltpu.VMEM((TOK // 2, 2 * RANK), F32),
            pltpu.VMEM((TOK // 2, 2 * RANK), F32),
            pltpu.VMEM((TOK // 2, 2 * RANK), BF16),
            pltpu.VMEM((2 * CHIPS, TOK // 2, 2 * RANK), BF16),
            dma, pair, pair, pair,
            pair, pair, pair, pair, chips, chips,
            each, each, halves, halves, halves, halves,
            halves, halves, halves, halves,
            each, each, chips, chips, pair, pair,
            dma((SPLIT,)), dma((SPLIT,)), dma((CHIPS,)), dma((CHIPS,)),
            dma, dma, dma((CHIPS,)), dma((CHIPS,)), dma, dma, dma((2 * CHIPS,)), dma((2 * CHIPS,)),
        ],
        compiler_params=pltpu.CompilerParams(
            collective_id=0, has_side_effects=True, vmem_limit_bytes=62 * 2**20
        ),
        cost_estimate=pl.CostEstimate(
            flops=8 * TOK * LAYERS * 1024 * COLS, bytes_accessed=6 * 2**20, transcendentals=0
        ),
    )(
        xd, xu, ad[0].T, au[0].T, bd[0], bu[0], chunks(wd), chunks(wu)
    )
    gad, gbd, gau, gbu = pl.pallas_call(
        gradients,
        out_shape=[jax.ShapeDtypeStruct((RANK, COLS), F32)] * 4,
        in_specs=[vmem] * 4,
        out_specs=[vmem] * 4,
        compiler_params=pltpu.CompilerParams(vmem_limit_bytes=62 * 2**20),
    )(*parts)
    return gad.T[None], gbd[None], gau.T[None], gbu[None]


def solution(mesh):
    in_specs = (
        P(None, None, "tensor"),
        P(None, None, "tensor"),
        P("section", "tensor", None),
        P("section", None, "tensor"),
        P("section", "tensor", None),
        P("section", None, "tensor"),
        P("section", None, "tensor"),
        P("section", None, "tensor"),
    )
    out_specs = (
        P("section", "tensor", None),
        P("section", None, "tensor"),
        P("section", "tensor", None),
        P("section", None, "tensor"),
    )
    return jax.shard_map(body, mesh=mesh, in_specs=in_specs, out_specs=out_specs, check_vma=False)
```

```python
import functools

import jax
import jax.numpy as jnp
from jax import lax
from jax.experimental import pallas as pl
from jax.experimental.pallas import tpu as pltpu
from jax.sharding import PartitionSpec as P

MESH = pl.DeviceIdType.MESH
F32, BF16 = jnp.float32, jnp.bfloat16
LAYERS = 4
CHIPS = 8
TOK = 64
COLS = 256
RANK = 64
SPLIT = 2
ROWS = TOK // SPLIT
SCALE = 2.0
FAR = (5, 7, 3, 4, 6, 2, 1)
NEAR = (0, 5, 7, 3, 4, 6, 2, 1)
WIDE = (11, 10, 9, 8, 15, 14, 7, 6, 13, 12, 5, 4, 3, 2, 1)


def nn(a, b):
    return jnp.dot(a, b, preferred_element_type=F32)


def nt(a, b):
    return lax.dot_general(a, b, (((1,), (1,)), ((), ())), preferred_element_type=F32)


def tn(a, b):
    return lax.dot_general(a, b, (((0,), (0,)), ((), ())), preferred_element_type=F32)


def fold(v):
    return jnp.concatenate([v[: TOK // 2], v[TOK // 2 :]], axis=1)


def unfold(v):
    return jnp.concatenate([v[:, :RANK], v[:, RANK:]], axis=0)


def kernel(
    xd, xu, atd, atu, bd, bu, wd, wu,
    c_out, g_out, h_out, e_out,
    w, weff, at, bch, hb, xs, xp, ts, tp, hs, hin, eb, ps, pr, eout, gs, gr, cs, cr, fs, fr,
    kept, b0, bp, us, ur, vs, vr,
    ld_x, ld_a, ld_b, ld_w,
    w_s, w_r, b_s, b_r, a_s, a_r, h_s, h_r, hx_s, hx_r, hc_s, hc_r,
    ec_s, ec_r, ex_s, ex_r, p_s, p_r, g_s, g_r, c_s, c_r, t_s, t_r, f_s, f_r,
    n_s, n_r, m_s, m_r, u_s, u_r, v_s, v_r,
):
    sec, t = lax.axis_index("section"), lax.axis_index("tensor")
    group, s = sec // LAYERS, sec % LAYERS
    chip, core = t // 2, t % 2
    low = s < 2
    q1 = jnp.where(low, s, LAYERS - 1 - s)
    toward = jnp.where(low, 1, -1)
    sibling = (sec, t ^ 1)

    def peer(m):
        return (sec, t ^ (2 * m))

    def rows(i):
        return pl.ds(i * ROWS, ROWS)

    def remote(src, dst, send, recv, to):
        return pltpu.make_async_remote_copy(
            src_ref=src, dst_ref=dst, send_sem=send, recv_sem=recv,
            device_id=to, device_id_type=MESH,
        )

    barrier = pltpu.get_barrier_semaphore()
    for m in FAR:
        pl.semaphore_signal(barrier, inc=1, device_id=peer(m), device_id_type=MESH)
    pl.semaphore_signal(barrier, inc=1, device_id=sibling, device_id_type=MESH)

    @pl.when(s > 0)
    def _():
        for other in (t, t ^ 1):
            pl.semaphore_signal(barrier, inc=1, device_id=(sec - 1, other), device_id_type=MESH)

    @pl.when(s < LAYERS - 1)
    def _():
        for other in (t, t ^ 1):
            pl.semaphore_signal(barrier, inc=1, device_id=(sec + 1, other), device_id_type=MESH)

    def start_local(r, down):
        x, a, b, v = (xd, atd, bd, wd) if down else (xu, atu, bu, wu)
        if r == 0:

            @pl.when(q1 == 0)
            def _():
                pltpu.make_async_copy(x.at[group], hb.at[0, 0], ld_x).start()

        pltpu.make_async_copy(a, at.at[r, 0], ld_a.at[r]).start()
        pltpu.make_async_copy(b, bch.at[r, 0], ld_b.at[r]).start()
        pltpu.make_async_copy(v.at[:, core], w.at[r, 0], ld_w.at[r]).start()

    @pl.when(low)
    def _():
        start_local(0, True)
        start_local(1, False)

    @pl.when(jnp.logical_not(low))
    def _():
        start_local(0, False)
        start_local(1, True)

    pl.semaphore_wait(barrier, jnp.where(q1 == 0, CHIPS + 2, CHIPS + 4))

    def h_copy(r, i, m):
        return remote(
            hb.at[r, 0, rows(i)], hb.at[r, m, rows(i)], h_s.at[r, i, m], h_r.at[r, i, m], peer(m)
        )

    def a_copy(r, m):
        return remote(at.at[r, 0], at.at[r, m], a_s.at[r, m], a_r.at[r, m], peer(m))

    def b_copy(r):
        return remote(bch.at[r, 0], bch.at[r, 1], b_s.at[r], b_r.at[r], sibling)

    def w_copy(r, down):
        v = wd if down else wu
        return remote(v.at[:, 1 - core], w.at[r, 1], w_s.at[r], w_r.at[r], sibling)

    @pl.when(q1 == 0)
    def _():
        pltpu.make_async_copy(xd.at[group], hb.at[0, 0], ld_x).wait()
        for m in FAR:
            h_copy(0, 0, m).start()

    def f_copy(m):
        return remote(fs, fr.at[m], f_s.at[m], f_r.at[m], peer(m))

    for r in range(2):
        pltpu.make_async_copy(atd, at.at[r, 0], ld_a.at[r]).wait()

    @pl.when(q1 == 0)
    def _():
        fs[...] = fold(SCALE * nt(hb[0, 0], at[0, 0]))
        for m in FAR:
            f_copy(m).start()
        for i in range(1, SPLIT):
            for m in FAR:
                h_copy(0, i, m).start()

    def share_lower(r):
        for m in FAR:
            a_copy(r, m).start()

    def share_weights(r):
        @pl.when(low == (r == 0))
        def _():
            w_copy(r, True).start()

        @pl.when(low != (r == 0))
        def _():
            w_copy(r, False).start()

        pltpu.make_async_copy(bd, bch.at[r, 0], ld_b.at[r]).wait()
        b_copy(r).start()

    share_weights(0)

    @pl.when(q1 == 1)
    def _():
        share_lower(0)
        share_weights(1)
        share_lower(1)

    def weights_here(r):
        b_copy(r).wait_recv()
        pltpu.make_async_copy(wd.at[:, core], w.at[r, 0], ld_w.at[r]).wait()
        w_copy(r, True).wait_recv()

    def combine_weights(r):
        for m in NEAR:
            if m:
                a_copy(r, m).wait_recv()
            j = chip ^ m
            for half in range(2):
                low_rank = tn(at[r, m], bch[r, half])
                weff[r, j, :, half * COLS : (half + 1) * COLS] = (
                    w[r, half, j].astype(F32) + SCALE * low_rank
                ).astype(BF16)

    def hx_copy(i):
        return remote(xs.at[rows(i)], xp.at[rows(i)], hx_s.at[i], hx_r.at[i], sibling)

    def hc_copy(r, i, half):
        to = (sec + toward if r == 0 else sec - toward, t ^ half)
        there = q1 if r == 0 else 1
        return remote(
            hs.at[r, half, rows(i)], hin.at[there, half, rows(i)],
            hc_s.at[r, half, i], hc_r.at[there, half, i], to,
        )

    def hc_arrived(r, i):
        for half in range(2):
            remote(
                hs.at[r, half, rows(i)], hin.at[r, half, rows(i)],
                hc_s.at[r, half, i], hc_r.at[r, half, i], sibling,
            ).wait_recv()
        piece = slice(i * ROWS, (i + 1) * ROWS)
        hb[r, 0, piece] = (
            hin[r, 0, piece].astype(F32) + hin[r, 1, piece].astype(F32)
        ).astype(BF16)

    def cross(r, i, half, value):
        hs[r, half, i * ROWS : (i + 1) * ROWS] = value.astype(BF16)
        hc_copy(r, i, half).start()

    def gather(r):
        for i in range(SPLIT):
            hc_arrived(r, i)
            for m in FAR:
                h_copy(r, i, m).start()

    def t_copy(i):
        return remote(ts.at[rows(i)], tp.at[rows(i)], t_s.at[i], t_r.at[i], sibling)

    def first_layer():
        for i in range(SPLIT):
            piece = slice(i * ROWS, (i + 1) * ROWS)
            other = jnp.zeros((ROWS, COLS), F32)
            for m in NEAR:
                if m:
                    h_copy(0, i, m).wait_recv()
                other = other + nn(hb[0, m, piece], w[0, 1, chip ^ m])
            if i == 0:
                lower = fs[...]
                for m in NEAR[1:]:
                    f_copy(m).wait_recv()
                    lower = lower + fr[m]
                cs[0] = lower
                c = unfold(lower).astype(BF16)
            other = other + nn(c[piece], bch[0, 1])
            cross(0, i, 1, other)
            own = nn(c[piece], bch[0, 0])
            for m in NEAR:
                own = own + nn(hb[0, m, piece], w[0, 0, chip ^ m])
            cross(0, i, 0, own + hb[0, 0, piece].astype(F32))
        c_copy(0).start()

    def later_layer(r, i, last):
        piece = slice(i * ROWS, (i + 1) * ROWS)
        total = jnp.zeros((ROWS, 2 * COLS), F32)
        for m in NEAR:
            if m:
                h_copy(r, i, m).wait_recv()
            total = total + nn(hb[r, m, piece], weff[r, chip ^ m])
        mine = hb[r, 0, piece].astype(F32) + total[:, :COLS]
        if not last:
            cross(r, i, 0, mine)
            cross(r, i, 1, total[:, COLS:])
            return
        xs[piece] = total[:, COLS:]
        hx_copy(i).start()
        ts[piece] = mine
        t_copy(i).start()
        hx_copy(i).wait_recv()
        eb[r, 0, piece] = (mine + xp[piece]).astype(BF16)
        t_copy(i).wait_recv()
        eb[r, 1, piece] = (total[:, COLS:] + tp[piece]).astype(BF16)

    def c_copy(r):
        return remote(cs.at[r], cr.at[r], c_s.at[r], c_r.at[r], sibling)

    def coefficients(r):
        total = nt(hb[r, 0], at[r, 0])
        for m in range(1, CHIPS):
            total = total + nt(hb[r, m], at[r, m])
        cs[r] = fold(SCALE * total)
        c_copy(r).start()

    def drain_forward(r, last=False):
        for i in range(SPLIT):
            for m in FAR:
                h_copy(r, i, m).wait_send()
            if last:
                hx_copy(i).wait_send()
                t_copy(i).wait_send()
            else:
                for half in range(2):
                    hc_copy(r, i, half).wait_send()

    def drain_weights(r):
        if r == 1:
            for m in FAR:
                a_copy(r, m).wait_send()
        b_copy(r).wait_send()
        w_copy(r, True).wait_send()

    def ec_copy(r, i):
        to = (sec - toward, t) if r == 0 else (sec + toward, t)
        there = 0 if r == 0 else 1 - q1
        return remote(
            eout.at[r, rows(i)], eb.at[there, 0, rows(i)], ec_s.at[r, i], ec_r.at[there, i], to
        )

    def ec_arrived(r, i):
        remote(
            eout.at[r, rows(i)], eb.at[r, 0, rows(i)], ec_s.at[r, i], ec_r.at[r, i], sibling
        ).wait_recv()

    def ex_copy(i):
        return remote(
            eout.at[1, rows(i)], eb.at[1 - q1, 1, rows(i)], ex_s.at[i], ex_r.at[1 - q1, i],
            (sec + toward, t ^ 1),
        )

    def ex_arrived(r, i):
        remote(
            eout.at[r, rows(i)], eb.at[r, 1, rows(i)], ex_s.at[i], ex_r.at[r, i], sibling
        ).wait_recv()

    def p_copy(r, i, m):
        return remote(
            ps.at[r, m, rows(i)], pr.at[r, m, rows(i)], p_s.at[r, i, m], p_r.at[r, i, m], peer(m)
        )

    def g_copy(r, m):
        return remote(gs.at[r], gr.at[r, m], g_s.at[r, m], g_r.at[r, m], peer(m))

    def sum_g(r):
        total = nt(eb[r, 0], bch[r, 0]) + nt(eb[r, 1], bch[r, 1])
        gs[r] = fold(total)
        for m in FAR:
            g_copy(r, m).start()

    def backward_out(r, i, turn):
        piece = slice(i * ROWS, (i + 1) * ROWS)
        if not turn:
            ec_arrived(r, i)
        e_own = eb[r, 0, piece]
        parts = [nt(e_own, weff[r, chip ^ m, :, :COLS]) for m in FAR + (0,)]
        if not turn:
            ex_arrived(r, i)
        e_other = eb[r, 1, piece]
        for m, part in zip(FAR + (0,), parts):
            part = part + nt(e_other, weff[r, chip ^ m, :, COLS:])
            if m:
                ps[r, m, piece] = part.astype(BF16)
                p_copy(r, i, m).start()
            else:
                kept[r, piece] = part + e_own.astype(F32)

    def backward_in(r, i):
        piece = slice(i * ROWS, (i + 1) * ROWS)
        total = kept[r, piece]
        for m in NEAR[1:]:
            p_copy(r, i, m).wait_recv()
            total = total + pr[r, m, piece].astype(F32)
        eout[r, piece] = total.astype(BF16)
        ec_copy(r, i).start()
        if r == 1:
            ex_copy(i).start()

    def drain_backward(r):
        for i in range(SPLIT):
            for m in FAR:
                p_copy(r, i, m).wait_send()
            ec_copy(r, i).wait_send()

    def n_copy():
        return remote(bch.at[0, 0], b0.at[0], n_s, n_r, (sec + toward, t))

    def m_copy(m):
        return remote(b0.at[0], b0.at[m], m_s.at[m], m_r.at[m], peer(m))

    def u_copy():
        return remote(us, ur, u_s, u_r, (sec - toward, t))

    def v_copy(n):
        return remote(vs, vr.at[n], v_s.at[n], v_r.at[n], (sec, t ^ n))

    def prepare_ahead():
        remote(bch.at[0, 0], b0.at[0], n_s, n_r, sibling).wait_recv()
        for m in FAR:
            m_copy(m).start()
        own, other = b0[0].astype(F32), jnp.zeros((RANK, COLS), F32)
        for m in NEAR:
            if m:
                m_copy(m).wait_recv()
            own = own + nn(b0[m], weff[0, chip ^ m, :, :COLS])
            other = other + nn(b0[m], weff[0, chip ^ m, :, COLS:])
        bp[0] = own.astype(BF16)
        bp[1] = other.astype(BF16)
        for m in FAR:
            m_copy(m).wait_send()

    def send_ahead():
        us[...] = fold(nt(eb[0, 0], bp[0]) + nt(eb[0, 1], bp[1]))
        u_copy().start()

    def receive_ahead():
        remote(us, ur, u_s, u_r, sibling).wait_recv()
        vs[...] = ur[...].astype(BF16)
        for n in WIDE:
            v_copy(n).start()
        total = ur[...]
        for n in reversed(WIDE):
            v_copy(n).wait_recv()
            total = total + vr[n].astype(F32)
        g_out[0] = unfold(total).astype(BF16)

    def keep(r):
        c_copy(r).wait_recv()
        c_out[r] = unfold(cs[r] + cr[r]).astype(BF16)
        h_out[r] = hb[r, 0]

    def finish(r):
        total = gs[r]
        for m in NEAR[1:]:
            g_copy(r, m).wait_recv()
            total = total + gr[r, m]
        g_out[r] = unfold(total).astype(BF16)
        e_out[r] = eb[r, 0]

    def close_forward():
        drain_weights(0)
        drain_weights(1)
        drain_forward(0)
        keep(0)

    def close_backward(r):
        finish(r)
        drain_backward(r)
        for m in FAR:
            g_copy(r, m).wait_send()

    @pl.when(q1 == 0)
    def _():
        weights_here(0)
        first_layer()
        share_weights(1)
        n_copy().start()
        share_lower(1)
        for m in FAR:
            f_copy(m).wait_send()
        weights_here(1)
        combine_weights(1)
        n_copy().wait_send()
        close_forward()
        gather(1)
        for i in range(SPLIT):
            later_layer(1, i, True)
            backward_out(1, i, True)
        for i in range(SPLIT):
            backward_in(1, i)
        sum_g(1)
        coefficients(1)
        drain_forward(1, True)
        keep(1)
        close_backward(1)
        receive_ahead()
        for n in WIDE:
            v_copy(n).wait_send()
        for i in range(SPLIT):
            ec_arrived(0, i)
        e_out[0] = eb[0, 0]

    @pl.when(q1 == 1)
    def _():
        weights_here(0)
        combine_weights(0)
        gather(0)
        weights_here(1)
        combine_weights(1)
        for i in range(SPLIT):
            later_layer(0, i, False)
        gather(1)
        coefficients(0)
        for m in FAR:
            a_copy(0, m).wait_send()
        close_forward()
        for i in range(SPLIT):
            later_layer(1, i, False)
        prepare_ahead()
        coefficients(1)
        drain_forward(1)
        keep(1)
        for i in range(SPLIT):
            backward_out(1, i, False)
        for i in range(SPLIT):
            backward_in(1, i)
        sum_g(1)
        for i in range(SPLIT):
            backward_out(0, i, False)
        send_ahead()
        close_backward(1)
        for i in range(SPLIT):
            backward_in(0, i)
        sum_g(0)
        close_backward(0)
        u_copy().wait_send()

    for i in range(SPLIT):
        ex_copy(i).wait_send()
    for r in range(2):
        c_copy(r).wait_send()


def gradients(c, g, h, e, gad, gbd, gau, gbu):
    low = lax.axis_index("section") % LAYERS < 2
    grad_a = [SCALE * tn(g[r], h[r]) for r in range(2)]
    grad_b = [tn(c[r], e[r]) for r in range(2)]

    @pl.when(low)
    def _():
        gad[...], gbd[...], gau[...], gbu[...] = grad_a[0], grad_b[0], grad_a[1], grad_b[1]

    @pl.when(jnp.logical_not(low))
    def _():
        gad[...], gbd[...], gau[...], gbu[...] = grad_a[1], grad_b[1], grad_a[0], grad_b[0]


def body(xd, xu, ad, bd, au, bu, wd, wu):
    def chunks(v):
        return v.reshape(CHIPS, 2, COLS, COLS)

    dma = pltpu.SemaphoreType.DMA
    anywhere = pl.BlockSpec(memory_space=pltpu.HBM)
    vmem = pl.BlockSpec(memory_space=pltpu.VMEM)
    pair = dma((2,))
    halves = dma((2, SPLIT))
    each = dma((2, SPLIT, CHIPS))
    chips = dma((2, CHIPS))
    parts = pl.pallas_call(
        kernel,
        out_shape=[jax.ShapeDtypeStruct((2, TOK, n), BF16) for n in (RANK, RANK, COLS, COLS)],
        in_specs=[anywhere] * 8,
        out_specs=[vmem] * 4,
        scratch_shapes=[
            pltpu.VMEM((2, 2, CHIPS, COLS, COLS), BF16),
            pltpu.VMEM((2, CHIPS, COLS, 2 * COLS), BF16),
            pltpu.VMEM((2, CHIPS, RANK, COLS), BF16),
            pltpu.VMEM((2, 2, RANK, COLS), BF16),
            pltpu.VMEM((2, CHIPS, TOK, COLS), BF16),
            pltpu.VMEM((TOK, COLS), F32),
            pltpu.VMEM((TOK, COLS), F32),
            pltpu.VMEM((TOK, COLS), F32),
            pltpu.VMEM((TOK, COLS), F32),
            pltpu.VMEM((2, 2, TOK, COLS), BF16),
            pltpu.VMEM((2, 2, TOK, COLS), BF16),
            pltpu.VMEM((2, 2, TOK, COLS), BF16),
            pltpu.VMEM((2, CHIPS, TOK, COLS), BF16),
            pltpu.VMEM((2, CHIPS, TOK, COLS), BF16),
            pltpu.VMEM((2, TOK, COLS), BF16),
            pltpu.VMEM((2, TOK // 2, 2 * RANK), F32),
            pltpu.VMEM((2, CHIPS, TOK // 2, 2 * RANK), F32),
            pltpu.VMEM((2, TOK // 2, 2 * RANK), F32),
            pltpu.VMEM((2, TOK // 2, 2 * RANK), F32),
            pltpu.VMEM((TOK // 2, 2 * RANK), F32),
            pltpu.VMEM((CHIPS, TOK // 2, 2 * RANK), F32),
            pltpu.VMEM((2, TOK, COLS), F32),
            pltpu.VMEM((CHIPS, RANK, COLS), BF16),
            pltpu.VMEM((2, RANK, COLS), BF16),
            pltpu.VMEM((TOK // 2, 2 * RANK), F32),
            pltpu.VMEM((TOK // 2, 2 * RANK), F32),
            pltpu.VMEM((TOK // 2, 2 * RANK), BF16),
            pltpu.VMEM((2 * CHIPS, TOK // 2, 2 * RANK), BF16),
            dma, pair, pair, pair,
            pair, pair, pair, pair, chips, chips,
            each, each, dma((SPLIT,)), dma((SPLIT,)), dma((2, 2, SPLIT)), dma((2, 2, SPLIT)),
            halves, halves, dma((SPLIT,)), halves,
            each, each, chips, chips, pair, pair,
            dma((SPLIT,)), dma((SPLIT,)), dma((CHIPS,)), dma((CHIPS,)),
            dma, dma, dma((CHIPS,)), dma((CHIPS,)), dma, dma, dma((2 * CHIPS,)), dma((2 * CHIPS,)),
        ],
        compiler_params=pltpu.CompilerParams(
            collective_id=0, has_side_effects=True, vmem_limit_bytes=62 * 2**20
        ),
        cost_estimate=pl.CostEstimate(
            flops=8 * TOK * LAYERS * 1024 * COLS, bytes_accessed=6 * 2**20, transcendentals=0
        ),
    )(
        xd, xu, ad[0].T, au[0].T, bd[0], bu[0], chunks(wd), chunks(wu)
    )
    gad, gbd, gau, gbu = pl.pallas_call(
        gradients,
        out_shape=[jax.ShapeDtypeStruct((RANK, COLS), F32)] * 4,
        in_specs=[vmem] * 4,
        out_specs=[vmem] * 4,
        compiler_params=pltpu.CompilerParams(vmem_limit_bytes=62 * 2**20),
    )(*parts)
    return gad.T[None], gbd[None], gau.T[None], gbu[None]


def solution(mesh):
    in_specs = (
        P(None, None, "tensor"),
        P(None, None, "tensor"),
        P("section", "tensor", None),
        P("section", None, "tensor"),
        P("section", "tensor", None),
        P("section", None, "tensor"),
        P("section", None, "tensor"),
        P("section", None, "tensor"),
    )
    out_specs = (
        P("section", "tensor", None),
        P("section", None, "tensor"),
        P("section", "tensor", None),
        P("section", None, "tensor"),
    )
    return jax.shard_map(body, mesh=mesh, in_specs=in_specs, out_specs=out_specs, check_vma=False)
```

```python
import functools

import jax
import jax.numpy as jnp
from jax import lax
from jax.experimental import pallas as pl
from jax.experimental.pallas import tpu as pltpu
from jax.sharding import PartitionSpec as P

MESH = pl.DeviceIdType.MESH
F32, BF16 = jnp.float32, jnp.bfloat16
LAYERS = 4
CHIPS = 8
TOK = 64
COLS = 256
RANK = 64
SPLIT = 2
ROWS = TOK // SPLIT
SCALE = 2.0
FAR = (5, 7, 3, 4, 6, 2, 1)
NEAR = (0, 5, 7, 3, 4, 6, 2, 1)
WIDE = (11, 10, 9, 8, 15, 14, 7, 6, 13, 12, 5, 4, 3, 2, 1)


def nn(a, b):
    return jnp.dot(a, b, preferred_element_type=F32)


def nt(a, b):
    return lax.dot_general(a, b, (((1,), (1,)), ((), ())), preferred_element_type=F32)


def tn(a, b):
    return lax.dot_general(a, b, (((0,), (0,)), ((), ())), preferred_element_type=F32)


def fold(v):
    return jnp.concatenate([v[: TOK // 2], v[TOK // 2 :]], axis=1)


def unfold(v):
    return jnp.concatenate([v[:, :RANK], v[:, RANK:]], axis=0)


def kernel(
    xd, xu, atd, atu, bd, bu, wd, wu,
    c_out, g_out, h_out, e_out,
    w, weff, at, bch, hb, xs, xp, ts, tp, hs, hin, eb, ps, pr, eout, gs, gr, cs, cr, fs, fr,
    kept, b0, bp, us, ur, vs, vr,
    ld_x, ld_a, ld_b, ld_w,
    w_s, w_r, b_s, b_r, a_s, a_r, h_s, h_r, hx_s, hx_r, hc_s, hc_r,
    ec_s, ec_r, ex_s, ex_r, p_s, p_r, g_s, g_r, c_s, c_r, t_s, t_r, f_s, f_r,
    n_s, n_r, m_s, m_r, u_s, u_r, v_s, v_r,
):
    sec, t = lax.axis_index("section"), lax.axis_index("tensor")
    group, s = sec // LAYERS, sec % LAYERS
    chip, core = t // 2, t % 2
    low = s < 2
    q1 = jnp.where(low, s, LAYERS - 1 - s)
    toward = jnp.where(low, 1, -1)
    sibling = (sec, t ^ 1)

    def peer(m):
        return (sec, t ^ (2 * m))

    def rows(i):
        return pl.ds(i * ROWS, ROWS)

    def remote(src, dst, send, recv, to):
        return pltpu.make_async_remote_copy(
            src_ref=src, dst_ref=dst, send_sem=send, recv_sem=recv,
            device_id=to, device_id_type=MESH,
        )

    barrier = pltpu.get_barrier_semaphore()
    for m in FAR:
        pl.semaphore_signal(barrier, inc=1, device_id=peer(m), device_id_type=MESH)
    pl.semaphore_signal(barrier, inc=1, device_id=sibling, device_id_type=MESH)

    @pl.when(s > 0)
    def _():
        for other in (t, t ^ 1):
            pl.semaphore_signal(barrier, inc=1, device_id=(sec - 1, other), device_id_type=MESH)

    @pl.when(s < LAYERS - 1)
    def _():
        for other in (t, t ^ 1):
            pl.semaphore_signal(barrier, inc=1, device_id=(sec + 1, other), device_id_type=MESH)

    def every(ref, send, recv):
        return remote(ref, ref, send, recv, sibling)

    others = pl.ds(1, CHIPS - 1)

    def all_h(r):
        return every(hb.at[r, others], h_s.at[r], h_r.at[r, 0, 0])

    def all_a(r):
        return every(at.at[r, others], a_s.at[r], a_r.at[r])

    def all_f():
        return every(fr.at[others], f_s, f_r)

    def all_p(r):
        return every(ps.at[r, others], p_s.at[r], p_r.at[r, 0])

    def all_p_in(r, i):
        return every(pr.at[r, others, rows(i)], p_s.at[r], p_r.at[r, i])

    def all_g(r):
        return every(gr.at[r, others], g_s.at[r], g_r.at[r])

    def all_m():
        return every(b0.at[others], m_s, m_r)

    def all_v():
        return every(vr.at[pl.ds(1, 2 * CHIPS - 1)], v_s, v_r)

    def start_local(r, down):
        x, a, b, v = (xd, atd, bd, wd) if down else (xu, atu, bu, wu)
        if r == 0:

            @pl.when(q1 == 0)
            def _():
                pltpu.make_async_copy(x.at[group], hb.at[0, 0], ld_x).start()

        pltpu.make_async_copy(a, at.at[r, 0], ld_a.at[r]).start()
        pltpu.make_async_copy(b, bch.at[r, 0], ld_b.at[r]).start()
        pltpu.make_async_copy(v.at[:, core], w.at[r, 0], ld_w.at[r]).start()

    @pl.when(low)
    def _():
        start_local(0, True)
        start_local(1, False)

    @pl.when(jnp.logical_not(low))
    def _():
        start_local(0, False)
        start_local(1, True)

    pl.semaphore_wait(barrier, jnp.where(q1 == 0, CHIPS + 2, CHIPS + 4))

    def h_copy(r, i, m):
        return remote(
            hb.at[r, 0, rows(i)], hb.at[r, m, rows(i)], h_s.at[r], h_r.at[r, i, m], peer(m)
        )

    def a_copy(r, m):
        return remote(at.at[r, 0], at.at[r, m], a_s.at[r], a_r.at[r], peer(m))

    def b_copy(r):
        return remote(bch.at[r, 0], bch.at[r, 1], b_s.at[r], b_r.at[r], sibling)

    def w_copy(r, down):
        v = wd if down else wu
        return remote(v.at[:, 1 - core], w.at[r, 1], w_s.at[r], w_r.at[r], sibling)

    @pl.when(q1 == 0)
    def _():
        pltpu.make_async_copy(xd.at[group], hb.at[0, 0], ld_x).wait()
        for m in FAR:
            h_copy(0, 0, m).start()

    def f_copy(m):
        return remote(fs, fr.at[m], f_s, f_r, peer(m))

    for r in range(2):
        pltpu.make_async_copy(atd, at.at[r, 0], ld_a.at[r]).wait()

    @pl.when(q1 == 0)
    def _():
        fs[...] = fold(SCALE * nt(hb[0, 0], at[0, 0]))
        for m in FAR:
            f_copy(m).start()
        for i in range(1, SPLIT):
            for m in FAR:
                h_copy(0, i, m).start()

    def share_lower(r):
        for m in FAR:
            a_copy(r, m).start()

    def share_weights(r):
        @pl.when(low == (r == 0))
        def _():
            w_copy(r, True).start()

        @pl.when(low != (r == 0))
        def _():
            w_copy(r, False).start()

        pltpu.make_async_copy(bd, bch.at[r, 0], ld_b.at[r]).wait()
        b_copy(r).start()

    share_weights(0)

    @pl.when(q1 == 1)
    def _():
        share_lower(0)
        share_weights(1)
        share_lower(1)

    def weights_here(r):
        b_copy(r).wait_recv()
        pltpu.make_async_copy(wd.at[:, core], w.at[r, 0], ld_w.at[r]).wait()
        w_copy(r, True).wait_recv()

    def combine_weights(r):
        all_a(r).wait_recv()
        for m in NEAR:
            j = chip ^ m
            for half in range(2):
                low_rank = tn(at[r, m], bch[r, half])
                weff[r, j, :, half * COLS : (half + 1) * COLS] = (
                    w[r, half, j].astype(F32) + SCALE * low_rank
                ).astype(BF16)

    def hx_copy(i):
        return remote(xs.at[rows(i)], xp.at[rows(i)], hx_s.at[i], hx_r.at[i], sibling)

    def hc_copy(r, i, half):
        to = (sec + toward if r == 0 else sec - toward, t ^ half)
        there = q1 if r == 0 else 1
        return remote(
            hs.at[r, half, rows(i)], hin.at[there, half, rows(i)],
            hc_s.at[r, half, i], hc_r.at[there, half, i], to,
        )

    def hc_arrived(r, i):
        for half in range(2):
            remote(
                hs.at[r, half, rows(i)], hin.at[r, half, rows(i)],
                hc_s.at[r, half, i], hc_r.at[r, half, i], sibling,
            ).wait_recv()
        piece = slice(i * ROWS, (i + 1) * ROWS)
        hb[r, 0, piece] = (
            hin[r, 0, piece].astype(F32) + hin[r, 1, piece].astype(F32)
        ).astype(BF16)

    def cross(r, i, half, value):
        hs[r, half, i * ROWS : (i + 1) * ROWS] = value.astype(BF16)
        hc_copy(r, i, half).start()

    def gather(r):
        for i in range(SPLIT):
            hc_arrived(r, i)
            for m in FAR:
                h_copy(r, i, m).start()

    def t_copy(i):
        return remote(ts.at[rows(i)], tp.at[rows(i)], t_s.at[i], t_r.at[i], sibling)

    def first_layer():
        for i in range(SPLIT):
            piece = slice(i * ROWS, (i + 1) * ROWS)
            other = jnp.zeros((ROWS, COLS), F32)
            for m in NEAR:
                if m:
                    h_copy(0, i, m).wait_recv()
                other = other + nn(hb[0, m, piece], w[0, 1, chip ^ m])
            if i == 0:
                lower = fs[...]
                all_f().wait_recv()
                for m in NEAR[1:]:
                    lower = lower + fr[m]
                cs[0] = lower
                c = unfold(lower).astype(BF16)
            other = other + nn(c[piece], bch[0, 1])
            cross(0, i, 1, other)
            own = nn(c[piece], bch[0, 0])
            for m in NEAR:
                own = own + nn(hb[0, m, piece], w[0, 0, chip ^ m])
            cross(0, i, 0, own + hb[0, 0, piece].astype(F32))
        c_copy(0).start()

    def later_layer(r, i, last):
        piece = slice(i * ROWS, (i + 1) * ROWS)
        total = jnp.zeros((ROWS, 2 * COLS), F32)
        for m in NEAR:
            if m:
                h_copy(r, i, m).wait_recv()
            total = total + nn(hb[r, m, piece], weff[r, chip ^ m])
        mine = hb[r, 0, piece].astype(F32) + total[:, :COLS]
        if not last:
            cross(r, i, 0, mine)
            cross(r, i, 1, total[:, COLS:])
            return
        xs[piece] = total[:, COLS:]
        hx_copy(i).start()
        ts[piece] = mine
        t_copy(i).start()
        hx_copy(i).wait_recv()
        eb[r, 0, piece] = (mine + xp[piece]).astype(BF16)
        t_copy(i).wait_recv()
        eb[r, 1, piece] = (total[:, COLS:] + tp[piece]).astype(BF16)

    def c_copy(r):
        return remote(cs.at[r], cr.at[r], c_s.at[r], c_r.at[r], sibling)

    def coefficients(r):
        total = nt(hb[r, 0], at[r, 0])
        for m in range(1, CHIPS):
            total = total + nt(hb[r, m], at[r, m])
        cs[r] = fold(SCALE * total)
        c_copy(r).start()

    def drain_forward(r, last=False):
        all_h(r).wait_send()
        for i in range(SPLIT):
            if last:
                hx_copy(i).wait_send()
                t_copy(i).wait_send()
            else:
                for half in range(2):
                    hc_copy(r, i, half).wait_send()

    def drain_weights(r):
        if r == 1:
            all_a(r).wait_send()
        b_copy(r).wait_send()
        w_copy(r, True).wait_send()

    def ec_copy(r, i):
        to = (sec - toward, t) if r == 0 else (sec + toward, t)
        there = 0 if r == 0 else 1 - q1
        return remote(
            eout.at[r, rows(i)], eb.at[there, 0, rows(i)], ec_s.at[r, i], ec_r.at[there, i], to
        )

    def ec_arrived(r, i):
        remote(
            eout.at[r, rows(i)], eb.at[r, 0, rows(i)], ec_s.at[r, i], ec_r.at[r, i], sibling
        ).wait_recv()

    def ex_copy(i):
        return remote(
            eout.at[1, rows(i)], eb.at[1 - q1, 1, rows(i)], ex_s.at[i], ex_r.at[1 - q1, i],
            (sec + toward, t ^ 1),
        )

    def ex_arrived(r, i):
        remote(
            eout.at[r, rows(i)], eb.at[r, 1, rows(i)], ex_s.at[i], ex_r.at[r, i], sibling
        ).wait_recv()

    def p_copy(r, i, m):
        return remote(
            ps.at[r, m, rows(i)], pr.at[r, m, rows(i)], p_s.at[r], p_r.at[r, i], peer(m)
        )

    def g_copy(r, m):
        return remote(gs.at[r], gr.at[r, m], g_s.at[r], g_r.at[r], peer(m))

    def sum_g(r):
        total = nt(eb[r, 0], bch[r, 0]) + nt(eb[r, 1], bch[r, 1])
        gs[r] = fold(total)
        for m in FAR:
            g_copy(r, m).start()

    def backward_out(r, i, turn):
        piece = slice(i * ROWS, (i + 1) * ROWS)
        if not turn:
            ec_arrived(r, i)
        e_own = eb[r, 0, piece]
        parts = [nt(e_own, weff[r, chip ^ m, :, :COLS]) for m in FAR + (0,)]
        if not turn:
            ex_arrived(r, i)
        e_other = eb[r, 1, piece]
        for m, part in zip(FAR + (0,), parts):
            part = part + nt(e_other, weff[r, chip ^ m, :, COLS:])
            if m:
                ps[r, m, piece] = part.astype(BF16)
                p_copy(r, i, m).start()
            else:
                kept[r, piece] = part + e_own.astype(F32)

    def backward_in(r, i):
        piece = slice(i * ROWS, (i + 1) * ROWS)
        total = kept[r, piece]
        all_p_in(r, i).wait_recv()
        for m in NEAR[1:]:
            total = total + pr[r, m, piece].astype(F32)
        eout[r, piece] = total.astype(BF16)
        ec_copy(r, i).start()
        if r == 1:
            ex_copy(i).start()

    def drain_backward(r):
        all_p(r).wait_send()
        for i in range(SPLIT):
            ec_copy(r, i).wait_send()

    def n_copy():
        return remote(bch.at[0, 0], b0.at[0], n_s, n_r, (sec + toward, t))

    def m_copy(m):
        return remote(b0.at[0], b0.at[m], m_s, m_r, peer(m))

    def u_copy():
        return remote(us, ur, u_s, u_r, (sec - toward, t))

    def v_copy(n):
        return remote(vs, vr.at[n], v_s, v_r, (sec, t ^ n))

    def prepare_ahead():
        remote(bch.at[0, 0], b0.at[0], n_s, n_r, sibling).wait_recv()
        for m in FAR:
            m_copy(m).start()
        own, other = b0[0].astype(F32), jnp.zeros((RANK, COLS), F32)
        all_m().wait_recv()
        for m in NEAR:
            own = own + nn(b0[m], weff[0, chip ^ m, :, :COLS])
            other = other + nn(b0[m], weff[0, chip ^ m, :, COLS:])
        bp[0] = own.astype(BF16)
        bp[1] = other.astype(BF16)
        all_m().wait_send()

    def send_ahead():
        us[...] = fold(nt(eb[0, 0], bp[0]) + nt(eb[0, 1], bp[1]))
        u_copy().start()

    def receive_ahead():
        remote(us, ur, u_s, u_r, sibling).wait_recv()
        vs[...] = ur[...].astype(BF16)
        for n in WIDE:
            v_copy(n).start()
        total = ur[...]
        all_v().wait_recv()
        for n in reversed(WIDE):
            total = total + vr[n].astype(F32)
        g_out[0] = unfold(total).astype(BF16)

    def keep(r):
        c_copy(r).wait_recv()
        c_out[r] = unfold(cs[r] + cr[r]).astype(BF16)
        h_out[r] = hb[r, 0]

    def finish(r):
        total = gs[r]
        all_g(r).wait_recv()
        for m in NEAR[1:]:
            total = total + gr[r, m]
        g_out[r] = unfold(total).astype(BF16)
        e_out[r] = eb[r, 0]

    def close_forward():
        drain_weights(0)
        drain_weights(1)
        drain_forward(0)
        keep(0)

    def close_backward(r):
        finish(r)
        drain_backward(r)
        all_g(r).wait_send()

    @pl.when(q1 == 0)
    def _():
        weights_here(0)
        first_layer()
        share_weights(1)
        n_copy().start()
        share_lower(1)
        all_f().wait_send()
        weights_here(1)
        combine_weights(1)
        n_copy().wait_send()
        close_forward()
        gather(1)
        for i in range(SPLIT):
            later_layer(1, i, True)
            backward_out(1, i, True)
        for i in range(SPLIT):
            backward_in(1, i)
        sum_g(1)
        coefficients(1)
        drain_forward(1, True)
        keep(1)
        close_backward(1)
        receive_ahead()
        all_v().wait_send()
        for i in range(SPLIT):
            ec_arrived(0, i)
        e_out[0] = eb[0, 0]

    @pl.when(q1 == 1)
    def _():
        weights_here(0)
        combine_weights(0)
        gather(0)
        weights_here(1)
        combine_weights(1)
        for i in range(SPLIT):
            later_layer(0, i, False)
        gather(1)
        coefficients(0)
        all_a(0).wait_send()
        close_forward()
        for i in range(SPLIT):
            later_layer(1, i, False)
        prepare_ahead()
        coefficients(1)
        drain_forward(1)
        keep(1)
        for i in range(SPLIT):
            backward_out(1, i, False)
        for i in range(SPLIT):
            backward_in(1, i)
        sum_g(1)
        for i in range(SPLIT):
            backward_out(0, i, False)
        send_ahead()
        close_backward(1)
        for i in range(SPLIT):
            backward_in(0, i)
        sum_g(0)
        close_backward(0)
        u_copy().wait_send()

    for i in range(SPLIT):
        ex_copy(i).wait_send()
    for r in range(2):
        c_copy(r).wait_send()


def gradients(c, g, h, e, gad, gbd, gau, gbu):
    low = lax.axis_index("section") % LAYERS < 2
    grad_a = [SCALE * tn(g[r], h[r]) for r in range(2)]
    grad_b = [tn(c[r], e[r]) for r in range(2)]

    @pl.when(low)
    def _():
        gad[...], gbd[...], gau[...], gbu[...] = grad_a[0], grad_b[0], grad_a[1], grad_b[1]

    @pl.when(jnp.logical_not(low))
    def _():
        gad[...], gbd[...], gau[...], gbu[...] = grad_a[1], grad_b[1], grad_a[0], grad_b[0]


def body(xd, xu, ad, bd, au, bu, wd, wu):
    def chunks(v):
        return v.reshape(CHIPS, 2, COLS, COLS)

    dma = pltpu.SemaphoreType.DMA
    anywhere = pl.BlockSpec(memory_space=pltpu.HBM)
    vmem = pl.BlockSpec(memory_space=pltpu.VMEM)
    pair = dma((2,))
    halves = dma((2, SPLIT))
    each = dma((2, SPLIT, CHIPS))
    parts = pl.pallas_call(
        kernel,
        out_shape=[jax.ShapeDtypeStruct((2, TOK, n), BF16) for n in (RANK, RANK, COLS, COLS)],
        in_specs=[anywhere] * 8,
        out_specs=[vmem] * 4,
        scratch_shapes=[
            pltpu.VMEM((2, 2, CHIPS, COLS, COLS), BF16),
            pltpu.VMEM((2, CHIPS, COLS, 2 * COLS), BF16),
            pltpu.VMEM((2, CHIPS, RANK, COLS), BF16),
            pltpu.VMEM((2, 2, RANK, COLS), BF16),
            pltpu.VMEM((2, CHIPS, TOK, COLS), BF16),
            pltpu.VMEM((TOK, COLS), F32),
            pltpu.VMEM((TOK, COLS), F32),
            pltpu.VMEM((TOK, COLS), F32),
            pltpu.VMEM((TOK, COLS), F32),
            pltpu.VMEM((2, 2, TOK, COLS), BF16),
            pltpu.VMEM((2, 2, TOK, COLS), BF16),
            pltpu.VMEM((2, 2, TOK, COLS), BF16),
            pltpu.VMEM((2, CHIPS, TOK, COLS), BF16),
            pltpu.VMEM((2, CHIPS, TOK, COLS), BF16),
            pltpu.VMEM((2, TOK, COLS), BF16),
            pltpu.VMEM((2, TOK // 2, 2 * RANK), F32),
            pltpu.VMEM((2, CHIPS, TOK // 2, 2 * RANK), F32),
            pltpu.VMEM((2, TOK // 2, 2 * RANK), F32),
            pltpu.VMEM((2, TOK // 2, 2 * RANK), F32),
            pltpu.VMEM((TOK // 2, 2 * RANK), F32),
            pltpu.VMEM((CHIPS, TOK // 2, 2 * RANK), F32),
            pltpu.VMEM((2, TOK, COLS), F32),
            pltpu.VMEM((CHIPS, RANK, COLS), BF16),
            pltpu.VMEM((2, RANK, COLS), BF16),
            pltpu.VMEM((TOK // 2, 2 * RANK), F32),
            pltpu.VMEM((TOK // 2, 2 * RANK), F32),
            pltpu.VMEM((TOK // 2, 2 * RANK), BF16),
            pltpu.VMEM((2 * CHIPS, TOK // 2, 2 * RANK), BF16),
            dma, pair, pair, pair,
            pair, pair, pair, pair, pair, pair,
            pair, each, dma((SPLIT,)), dma((SPLIT,)), dma((2, 2, SPLIT)), dma((2, 2, SPLIT)),
            halves, halves, dma((SPLIT,)), halves,
            pair, halves, pair, pair, pair, pair,
            dma((SPLIT,)), dma((SPLIT,)), dma, dma,
            dma, dma, dma, dma, dma, dma, dma, dma,
        ],
        compiler_params=pltpu.CompilerParams(
            collective_id=0, has_side_effects=True, vmem_limit_bytes=62 * 2**20
        ),
        cost_estimate=pl.CostEstimate(
            flops=8 * TOK * LAYERS * 1024 * COLS, bytes_accessed=6 * 2**20, transcendentals=0
        ),
    )(
        xd, xu, ad[0].T, au[0].T, bd[0], bu[0], chunks(wd), chunks(wu)
    )
    gad, gbd, gau, gbu = pl.pallas_call(
        gradients,
        out_shape=[jax.ShapeDtypeStruct((RANK, COLS), F32)] * 4,
        in_specs=[vmem] * 4,
        out_specs=[vmem] * 4,
        compiler_params=pltpu.CompilerParams(vmem_limit_bytes=62 * 2**20),
    )(*parts)
    return gad.T[None], gbd[None], gau.T[None], gbu[None]


def solution(mesh):
    in_specs = (
        P(None, None, "tensor"),
        P(None, None, "tensor"),
        P("section", "tensor", None),
        P("section", None, "tensor"),
        P("section", "tensor", None),
        P("section", None, "tensor"),
        P("section", None, "tensor"),
        P("section", None, "tensor"),
    )
    out_specs = (
        P("section", "tensor", None),
        P("section", None, "tensor"),
        P("section", "tensor", None),
        P("section", None, "tensor"),
    )
    return jax.shard_map(body, mesh=mesh, in_specs=in_specs, out_specs=out_specs, check_vma=False)
```

```python
import functools

import jax
import jax.numpy as jnp
from jax import lax
from jax.experimental import pallas as pl
from jax.experimental.pallas import tpu as pltpu
from jax.sharding import PartitionSpec as P

MESH = pl.DeviceIdType.MESH
F32, BF16 = jnp.float32, jnp.bfloat16
LAYERS = 4
CHIPS = 8
TOK = 64
COLS = 256
RANK = 64
SPLIT = 2
ROWS = TOK // SPLIT
SCALE = 2.0
FAR = (5, 7, 3, 4, 6, 2, 1)
NEAR = (0, 5, 7, 3, 4, 6, 2, 1)
WIDE = (11, 10, 9, 8, 15, 14, 7, 6, 13, 12, 5, 4, 3, 2, 1)


def nn(a, b):
    return jnp.dot(a, b, preferred_element_type=F32)


def nt(a, b):
    return lax.dot_general(a, b, (((1,), (1,)), ((), ())), preferred_element_type=F32)


def tn(a, b):
    return lax.dot_general(a, b, (((0,), (0,)), ((), ())), preferred_element_type=F32)


def fold(v):
    return jnp.concatenate([v[: TOK // 2], v[TOK // 2 :]], axis=1)


def unfold(v):
    return jnp.concatenate([v[:, :RANK], v[:, RANK:]], axis=0)


def kernel(
    xd, xu, atd, atu, bd, bu, wd, wu,
    c_out, g_out, h_out, e_out,
    w, weff, weft, at, bch, hb, xs, xp, ts, tp, hs, hin, eb, ps, pr, eout, gs, gr, cs, cr, fs, fr,
    kept, b0, bp, us, ur, vs, vr,
    ld_x, ld_a, ld_b, ld_w,
    w_s, w_r, b_s, b_r, a_s, a_r, h_s, h_r, hx_s, hx_r, hc_s, hc_r,
    ec_s, ec_r, ex_s, ex_r, p_s, p_r, g_s, g_r, c_s, c_r, t_s, t_r, f_s, f_r,
    n_s, n_r, m_s, m_r, u_s, u_r, v_s, v_r,
):
    sec, t = lax.axis_index("section"), lax.axis_index("tensor")
    group, s = sec // LAYERS, sec % LAYERS
    chip, core = t // 2, t % 2
    low = s < 2
    q1 = jnp.where(low, s, LAYERS - 1 - s)
    toward = jnp.where(low, 1, -1)
    sibling = (sec, t ^ 1)

    def peer(m):
        return (sec, t ^ (2 * m))

    def rows(i):
        return pl.ds(i * ROWS, ROWS)

    def remote(src, dst, send, recv, to):
        return pltpu.make_async_remote_copy(
            src_ref=src, dst_ref=dst, send_sem=send, recv_sem=recv,
            device_id=to, device_id_type=MESH,
        )

    barrier = pltpu.get_barrier_semaphore()
    for m in FAR:
        pl.semaphore_signal(barrier, inc=1, device_id=peer(m), device_id_type=MESH)
    pl.semaphore_signal(barrier, inc=1, device_id=sibling, device_id_type=MESH)

    @pl.when(s > 0)
    def _():
        for other in (t, t ^ 1):
            pl.semaphore_signal(barrier, inc=1, device_id=(sec - 1, other), device_id_type=MESH)

    @pl.when(s < LAYERS - 1)
    def _():
        for other in (t, t ^ 1):
            pl.semaphore_signal(barrier, inc=1, device_id=(sec + 1, other), device_id_type=MESH)

    def every(ref, send, recv):
        return remote(ref, ref, send, recv, sibling)

    others = pl.ds(1, CHIPS - 1)

    def all_h(r):
        return every(hb.at[r, others], h_s.at[r], h_r.at[r, 0, 0])

    def all_a(r):
        return every(at.at[r, others], a_s.at[r], a_r.at[r])

    def all_f():
        return every(fr.at[others], f_s, f_r)

    def all_p(r):
        return every(ps.at[r, others], p_s.at[r], p_r.at[r, 0])

    def all_p_in(r, i):
        return every(pr.at[r, others, rows(i)], p_s.at[r], p_r.at[r, i])

    def all_g(r):
        return every(gr.at[r, others], g_s.at[r], g_r.at[r])

    def all_m():
        return every(b0.at[others], m_s, m_r)

    def all_v():
        return every(vr.at[pl.ds(1, 2 * CHIPS - 1)], v_s, v_r)

    def start_local(r, down):
        x, a, b, v = (xd, atd, bd, wd) if down else (xu, atu, bu, wu)
        if r == 0:

            @pl.when(q1 == 0)
            def _():
                pltpu.make_async_copy(x.at[group], hb.at[0, 0], ld_x).start()

        pltpu.make_async_copy(a, at.at[r, 0], ld_a.at[r]).start()
        pltpu.make_async_copy(b, bch.at[r, 0], ld_b.at[r]).start()
        pltpu.make_async_copy(v.at[:, core], w.at[r, 0], ld_w.at[r]).start()

    @pl.when(low)
    def _():
        start_local(0, True)
        start_local(1, False)

    @pl.when(jnp.logical_not(low))
    def _():
        start_local(0, False)
        start_local(1, True)

    pl.semaphore_wait(barrier, jnp.where(q1 == 0, CHIPS + 2, CHIPS + 4))

    def h_copy(r, i, m):
        return remote(
            hb.at[r, 0, rows(i)], hb.at[r, m, rows(i)], h_s.at[r], h_r.at[r, i, m], peer(m)
        )

    def a_copy(r, m):
        return remote(at.at[r, 0], at.at[r, m], a_s.at[r], a_r.at[r], peer(m))

    def b_copy(r):
        return remote(bch.at[r, 0], bch.at[r, 1], b_s.at[r], b_r.at[r], sibling)

    def w_copy(r, down):
        v = wd if down else wu
        return remote(v.at[:, 1 - core], w.at[r, 1], w_s.at[r], w_r.at[r], sibling)

    @pl.when(q1 == 0)
    def _():
        pltpu.make_async_copy(xd.at[group], hb.at[0, 0], ld_x).wait()
        for m in FAR:
            h_copy(0, 0, m).start()

    def f_copy(m):
        return remote(fs, fr.at[m], f_s, f_r, peer(m))

    for r in range(2):
        pltpu.make_async_copy(atd, at.at[r, 0], ld_a.at[r]).wait()

    @pl.when(q1 == 0)
    def _():
        fs[...] = fold(SCALE * nt(hb[0, 0], at[0, 0]))
        for m in FAR:
            f_copy(m).start()
        for i in range(1, SPLIT):
            for m in FAR:
                h_copy(0, i, m).start()

    def share_lower(r):
        for m in FAR:
            a_copy(r, m).start()

    def share_weights(r):
        @pl.when(low == (r == 0))
        def _():
            w_copy(r, True).start()

        @pl.when(low != (r == 0))
        def _():
            w_copy(r, False).start()

        pltpu.make_async_copy(bd, bch.at[r, 0], ld_b.at[r]).wait()
        b_copy(r).start()

    share_weights(0)

    @pl.when(q1 == 1)
    def _():
        share_lower(0)
        share_weights(1)
        share_lower(1)

    def weights_here(r):
        b_copy(r).wait_recv()
        pltpu.make_async_copy(wd.at[:, core], w.at[r, 0], ld_w.at[r]).wait()
        w_copy(r, True).wait_recv()

    def combine_weights(r):
        all_a(r).wait_recv()
        for m in NEAR:
            j = chip ^ m
            for half in range(2):
                low_rank = tn(at[r, m], bch[r, half])
                weff[r, j, :, half * COLS : (half + 1) * COLS] = (
                    w[r, half, j].astype(F32) + SCALE * low_rank
                ).astype(BF16)

    def hx_copy(i):
        return remote(xs.at[rows(i)], xp.at[rows(i)], hx_s.at[i], hx_r.at[i], sibling)

    def hc_copy(r, i, half):
        to = (sec + toward if r == 0 else sec - toward, t ^ half)
        there = q1 if r == 0 else 1
        return remote(
            hs.at[r, half, rows(i)], hin.at[there, half, rows(i)],
            hc_s.at[r], hc_r.at[there, i], to,
        )

    def hc_arrived(r, i):
        arrived = hin.at[r, :, rows(i)]
        every(arrived, hc_s.at[r], hc_r.at[r, i]).wait_recv()
        piece = slice(i * ROWS, (i + 1) * ROWS)
        hb[r, 0, piece] = (
            hin[r, 0, piece].astype(F32) + hin[r, 1, piece].astype(F32)
        ).astype(BF16)

    def cross(r, i, half, value):
        hs[r, half, i * ROWS : (i + 1) * ROWS] = value.astype(BF16)
        hc_copy(r, i, half).start()

    def gather(r):
        for i in range(SPLIT):
            hc_arrived(r, i)
            for m in FAR:
                h_copy(r, i, m).start()

    def t_copy(i):
        return remote(ts.at[rows(i)], tp.at[rows(i)], t_s.at[i], t_r.at[i], sibling)

    def first_layer():
        for i in range(SPLIT):
            piece = slice(i * ROWS, (i + 1) * ROWS)
            other = jnp.zeros((ROWS, COLS), F32)
            for m in NEAR:
                if m:
                    h_copy(0, i, m).wait_recv()
                other = other + nn(hb[0, m, piece], w[0, 1, chip ^ m])
            if i == 0:
                lower = fs[...]
                all_f().wait_recv()
                for m in NEAR[1:]:
                    lower = lower + fr[m]
                cs[0] = lower
                c = unfold(lower).astype(BF16)
            other = other + nn(c[piece], bch[0, 1])
            cross(0, i, 1, other)
            own = nn(c[piece], bch[0, 0])
            for m in NEAR:
                own = own + nn(hb[0, m, piece], w[0, 0, chip ^ m])
            cross(0, i, 0, own + hb[0, 0, piece].astype(F32))
        c_copy(0).start()

    def later_layer(r, i, last):
        piece = slice(i * ROWS, (i + 1) * ROWS)
        total = jnp.zeros((ROWS, 2 * COLS), F32)
        for m in NEAR:
            if m:
                h_copy(r, i, m).wait_recv()
            total = total + nn(hb[r, m, piece], weff[r, chip ^ m])
        mine = hb[r, 0, piece].astype(F32) + total[:, :COLS]
        if not last:
            cross(r, i, 0, mine)
            cross(r, i, 1, total[:, COLS:])
            return
        xs[piece] = total[:, COLS:]
        hx_copy(i).start()
        ts[piece] = mine
        t_copy(i).start()
        hx_copy(i).wait_recv()
        eb[r, 0, piece] = (mine + xp[piece]).astype(BF16)
        t_copy(i).wait_recv()
        eb[r, 1, piece] = (total[:, COLS:] + tp[piece]).astype(BF16)

    def c_copy(r):
        return remote(cs.at[r], cr.at[r], c_s.at[r], c_r.at[r], sibling)

    def coefficients(r):
        total = nt(hb[r, 0], at[r, 0])
        for m in range(1, CHIPS):
            total = total + nt(hb[r, m], at[r, m])
        cs[r] = fold(SCALE * total)
        c_copy(r).start()

    def drain_forward(r, last=False):
        all_h(r).wait_send()
        if last:
            for i in range(SPLIT):
                hx_copy(i).wait_send()
                t_copy(i).wait_send()
        else:
            every(hs.at[r], hc_s.at[r], hc_r.at[r, 0]).wait_send()

    def drain_weights(r):
        if r == 1:
            all_a(r).wait_send()
        b_copy(r).wait_send()
        w_copy(r, True).wait_send()

    def ec_copy(r, i):
        to = (sec - toward, t) if r == 0 else (sec + toward, t)
        there = 0 if r == 0 else 1 - q1
        return remote(
            eout.at[r, rows(i)], eb.at[there, 0, rows(i)], ec_s.at[r, i], ec_r.at[there, i], to
        )

    def ec_arrived(r, i):
        remote(
            eout.at[r, rows(i)], eb.at[r, 0, rows(i)], ec_s.at[r, i], ec_r.at[r, i], sibling
        ).wait_recv()

    def ex_copy(i):
        return remote(
            eout.at[1, rows(i)], eb.at[1 - q1, 1, rows(i)], ex_s.at[i], ex_r.at[1 - q1, i],
            (sec + toward, t ^ 1),
        )

    def ex_arrived(r, i):
        remote(
            eout.at[r, rows(i)], eb.at[r, 1, rows(i)], ex_s.at[i], ex_r.at[r, i], sibling
        ).wait_recv()

    def p_copy(r, i, m):
        return remote(
            ps.at[r, m, rows(i)], pr.at[r, m, rows(i)], p_s.at[r], p_r.at[r, i], peer(m)
        )

    def g_copy(r, m):
        return remote(gs.at[r], gr.at[r, m], g_s.at[r], g_r.at[r], peer(m))

    def sum_g(r):
        total = nt(eb[r, 0], bch[r, 0]) + nt(eb[r, 1], bch[r, 1])
        gs[r] = fold(total)
        for m in FAR:
            g_copy(r, m).start()

    def backward_out(r, i, turn):
        piece = slice(i * ROWS, (i + 1) * ROWS)
        if not turn:
            ec_arrived(r, i)
        e_own = eb[r, 0, piece]
        parts = [nn(e_own, weft[r, chip ^ m, :COLS]) for m in FAR + (0,)]
        if not turn:
            ex_arrived(r, i)
        e_other = eb[r, 1, piece]
        for m, part in zip(FAR + (0,), parts):
            part = part + nn(e_other, weft[r, chip ^ m, COLS:])
            if m:
                ps[r, m, piece] = part.astype(BF16)
                p_copy(r, i, m).start()
            else:
                kept[r, piece] = part + e_own.astype(F32)

    def backward_in(r, i):
        piece = slice(i * ROWS, (i + 1) * ROWS)
        total = kept[r, piece]
        all_p_in(r, i).wait_recv()
        for m in NEAR[1:]:
            total = total + pr[r, m, piece].astype(F32)
        eout[r, piece] = total.astype(BF16)
        ec_copy(r, i).start()
        if r == 1:
            ex_copy(i).start()

    def drain_backward(r):
        all_p(r).wait_send()
        for i in range(SPLIT):
            ec_copy(r, i).wait_send()

    def n_copy():
        return remote(bch.at[0, 0], b0.at[0], n_s, n_r, (sec + toward, t))

    def m_copy(m):
        return remote(b0.at[0], b0.at[m], m_s, m_r, peer(m))

    def u_copy():
        return remote(us, ur, u_s, u_r, (sec - toward, t))

    def v_copy(n):
        return remote(vs, vr.at[n], v_s, v_r, (sec, t ^ n))

    def transpose_weights(r):
        def one(j, _):
            weft[r, j] = weff[r, j].T
            return 0

        lax.fori_loop(0, CHIPS, one, 0)

    def prepare_ahead():
        remote(bch.at[0, 0], b0.at[0], n_s, n_r, sibling).wait_recv()
        for m in FAR:
            m_copy(m).start()
        own, other = b0[0].astype(F32), jnp.zeros((RANK, COLS), F32)
        all_m().wait_recv()
        for m in NEAR:
            own = own + nn(b0[m], weff[0, chip ^ m, :, :COLS])
            other = other + nn(b0[m], weff[0, chip ^ m, :, COLS:])
        bp[0] = own.astype(BF16)
        bp[1] = other.astype(BF16)
        all_m().wait_send()

    def send_ahead():
        us[...] = fold(nt(eb[0, 0], bp[0]) + nt(eb[0, 1], bp[1]))
        u_copy().start()

    def receive_ahead():
        remote(us, ur, u_s, u_r, sibling).wait_recv()
        vs[...] = ur[...].astype(BF16)
        for n in WIDE:
            v_copy(n).start()
        total = ur[...]
        all_v().wait_recv()
        for n in reversed(WIDE):
            total = total + vr[n].astype(F32)
        g_out[0] = unfold(total).astype(BF16)

    def keep(r):
        c_copy(r).wait_recv()
        c_out[r] = unfold(cs[r] + cr[r]).astype(BF16)
        h_out[r] = hb[r, 0]

    def finish(r):
        total = gs[r]
        all_g(r).wait_recv()
        for m in NEAR[1:]:
            total = total + gr[r, m]
        g_out[r] = unfold(total).astype(BF16)
        e_out[r] = eb[r, 0]

    def close_forward():
        drain_weights(0)
        drain_weights(1)
        drain_forward(0)
        keep(0)

    def close_backward(r):
        finish(r)
        drain_backward(r)
        all_g(r).wait_send()

    @pl.when(q1 == 0)
    def _():
        weights_here(0)
        first_layer()
        share_weights(1)
        n_copy().start()
        share_lower(1)
        all_f().wait_send()
        weights_here(1)
        combine_weights(1)
        transpose_weights(1)
        n_copy().wait_send()
        close_forward()
        gather(1)
        for i in range(SPLIT):
            later_layer(1, i, True)
            backward_out(1, i, True)
        for i in range(SPLIT):
            backward_in(1, i)
        sum_g(1)
        coefficients(1)
        drain_forward(1, True)
        keep(1)
        close_backward(1)
        receive_ahead()
        all_v().wait_send()
        for i in range(SPLIT):
            ec_arrived(0, i)
        e_out[0] = eb[0, 0]

    @pl.when(q1 == 1)
    def _():
        weights_here(0)
        combine_weights(0)
        gather(0)
        weights_here(1)
        combine_weights(1)
        for i in range(SPLIT):
            later_layer(0, i, False)
        gather(1)
        coefficients(0)
        all_a(0).wait_send()
        close_forward()
        for i in range(SPLIT):
            later_layer(1, i, False)
        prepare_ahead()
        transpose_weights(1)
        transpose_weights(0)
        coefficients(1)
        drain_forward(1)
        keep(1)
        for i in range(SPLIT):
            backward_out(1, i, False)
        for i in range(SPLIT):
            backward_in(1, i)
        sum_g(1)
        for i in range(SPLIT):
            backward_out(0, i, False)
        send_ahead()
        close_backward(1)
        for i in range(SPLIT):
            backward_in(0, i)
        sum_g(0)
        close_backward(0)
        u_copy().wait_send()

    for i in range(SPLIT):
        ex_copy(i).wait_send()
    for r in range(2):
        c_copy(r).wait_send()


def gradients(c, g, h, e, gad, gbd, gau, gbu):
    low = lax.axis_index("section") % LAYERS < 2
    grad_a = [SCALE * tn(g[r], h[r]) for r in range(2)]
    grad_b = [tn(c[r], e[r]) for r in range(2)]

    @pl.when(low)
    def _():
        gad[...], gbd[...], gau[...], gbu[...] = grad_a[0], grad_b[0], grad_a[1], grad_b[1]

    @pl.when(jnp.logical_not(low))
    def _():
        gad[...], gbd[...], gau[...], gbu[...] = grad_a[1], grad_b[1], grad_a[0], grad_b[0]


def body(xd, xu, ad, bd, au, bu, wd, wu):
    def chunks(v):
        return v.reshape(CHIPS, 2, COLS, COLS)

    dma = pltpu.SemaphoreType.DMA
    anywhere = pl.BlockSpec(memory_space=pltpu.HBM)
    vmem = pl.BlockSpec(memory_space=pltpu.VMEM)
    pair = dma((2,))
    halves = dma((2, SPLIT))
    each = dma((2, SPLIT, CHIPS))
    parts = pl.pallas_call(
        kernel,
        out_shape=[jax.ShapeDtypeStruct((2, TOK, n), BF16) for n in (RANK, RANK, COLS, COLS)],
        in_specs=[anywhere] * 8,
        out_specs=[vmem] * 4,
        scratch_shapes=[
            pltpu.VMEM((2, 2, CHIPS, COLS, COLS), BF16),
            pltpu.VMEM((2, CHIPS, COLS, 2 * COLS), BF16),
            pltpu.VMEM((2, CHIPS, 2 * COLS, COLS), BF16),
            pltpu.VMEM((2, CHIPS, RANK, COLS), BF16),
            pltpu.VMEM((2, 2, RANK, COLS), BF16),
            pltpu.VMEM((2, CHIPS, TOK, COLS), BF16),
            pltpu.VMEM((TOK, COLS), F32),
            pltpu.VMEM((TOK, COLS), F32),
            pltpu.VMEM((TOK, COLS), F32),
            pltpu.VMEM((TOK, COLS), F32),
            pltpu.VMEM((2, 2, TOK, COLS), BF16),
            pltpu.VMEM((2, 2, TOK, COLS), BF16),
            pltpu.VMEM((2, 2, TOK, COLS), BF16),
            pltpu.VMEM((2, CHIPS, TOK, COLS), BF16),
            pltpu.VMEM((2, CHIPS, TOK, COLS), BF16),
            pltpu.VMEM((2, TOK, COLS), BF16),
            pltpu.VMEM((2, TOK // 2, 2 * RANK), F32),
            pltpu.VMEM((2, CHIPS, TOK // 2, 2 * RANK), F32),
            pltpu.VMEM((2, TOK // 2, 2 * RANK), F32),
            pltpu.VMEM((2, TOK // 2, 2 * RANK), F32),
            pltpu.VMEM((TOK // 2, 2 * RANK), F32),
            pltpu.VMEM((CHIPS, TOK // 2, 2 * RANK), F32),
            pltpu.VMEM((2, TOK, COLS), F32),
            pltpu.VMEM((CHIPS, RANK, COLS), BF16),
            pltpu.VMEM((2, RANK, COLS), BF16),
            pltpu.VMEM((TOK // 2, 2 * RANK), F32),
            pltpu.VMEM((TOK // 2, 2 * RANK), F32),
            pltpu.VMEM((TOK // 2, 2 * RANK), BF16),
            pltpu.VMEM((2 * CHIPS, TOK // 2, 2 * RANK), BF16),
            dma, pair, pair, pair,
            pair, pair, pair, pair, pair, pair,
            pair, each, dma((SPLIT,)), dma((SPLIT,)), pair, halves,
            halves, halves, dma((SPLIT,)), halves,
            pair, halves, pair, pair, pair, pair,
            dma((SPLIT,)), dma((SPLIT,)), dma, dma,
            dma, dma, dma, dma, dma, dma, dma, dma,
        ],
        compiler_params=pltpu.CompilerParams(
            collective_id=0, has_side_effects=True, vmem_limit_bytes=62 * 2**20
        ),
        cost_estimate=pl.CostEstimate(
            flops=8 * TOK * LAYERS * 1024 * COLS, bytes_accessed=6 * 2**20, transcendentals=0
        ),
    )(
        xd, xu, ad[0].T, au[0].T, bd[0], bu[0], chunks(wd), chunks(wu)
    )
    gad, gbd, gau, gbu = pl.pallas_call(
        gradients,
        out_shape=[jax.ShapeDtypeStruct((RANK, COLS), F32)] * 4,
        in_specs=[vmem] * 4,
        out_specs=[vmem] * 4,
        compiler_params=pltpu.CompilerParams(vmem_limit_bytes=62 * 2**20),
    )(*parts)
    return gad.T[None], gbd[None], gau.T[None], gbu[None]


def solution(mesh):
    in_specs = (
        P(None, None, "tensor"),
        P(None, None, "tensor"),
        P("section", "tensor", None),
        P("section", None, "tensor"),
        P("section", "tensor", None),
        P("section", None, "tensor"),
        P("section", None, "tensor"),
        P("section", None, "tensor"),
    )
    out_specs = (
        P("section", "tensor", None),
        P("section", None, "tensor"),
        P("section", "tensor", None),
        P("section", None, "tensor"),
    )
    return jax.shard_map(body, mesh=mesh, in_specs=in_specs, out_specs=out_specs, check_vma=False)
```
